256 devices in a mesh: ctx: 16 (over y_lo, x, core), tp: 16 (over y_hi, z).
Axes of the slice: x: 4, y: 4 (y_hi: 2, y_lo: 2; y = y_hi * 2 + y_lo), z: 8, core: 2. Of those that a mesh axis runs over, the one named last changes fastest.
Arguments:
- latent: bfloat16 [2048, 5120], P('ctx', 'tp'), may hold values from -2.5 to 2.5
- noise_levels: int32 [3, 16], P(None, 'ctx'), may hold values from 0 to 31, as said below
- mod_table: float32 [32, 2, 5120], replicated, may hold values from -2.5 to 2.5
- w_query: bfloat16 [5120, 4096], P(None, 'tp'), may hold values from -0.078125 to 0.078125
- w_key: bfloat16 [5120, 4096], P(None, 'tp'), may hold values from -0.078125 to 0.078125
- w_value: bfloat16 [5120, 4096], P(None, 'tp'), may hold values from -0.078125 to 0.078125
- w_out: bfloat16 [4096, 5120], P('tp'), may hold values from -0.09375 to 0.09375
- hist_keys: bfloat16 [64, 128, 4096], P('ctx', None, 'tp'), may hold values from -102 to 102
- hist_values: bfloat16 [64, 128, 4096], P('ctx', None, 'tp'), may hold values from -6 to 6
- frame_home: int32 [64], replicated, may hold values from 0 to 63, as said below
- hist_list: int32 [16, 16], P('ctx'), may hold values from 0 to 63, as said below
- list_count: int32 [16], P('ctx'), may hold values from 8 to 16, as said below
Outputs:
- denoised: bfloat16 [2048, 5120], P('ctx', 'tp')
- velocities: bfloat16 [2, 2048, 5120], P(None, 'ctx', 'tp')
The draws below stay inside these ranges and needn't reach their ends.
Inputs may be any that keep to these rules, and one draw needn't show every extreme that they name: `noise_levels`: for each frame the level falls from each row to the next by 1 to 8. A permutation: frame f lies in slot frame_home[f], held by memory owner frame_home[f] // 4. `hist_list`: row b names, for each of the 16 memory owners, exactly one frame held by that owner; only the first list_count[b] entries are read. `list_count`: some query block reads its whole list.
All inputs are finite; a program needn't handle non-finite values.
Results may differ from the reference program's by a relative error of at most 0.04.
The reference program's roundings to bfloat16 on the way (of `normed`, `weights` and `attended`) count: a program that leaves them out, or rounds other values in their place, can miss the bound.
Values may be sent and summed in bfloat16 or wider, within the bound.
No kernel may reach another device: no remote copies, remote signals or barrier semaphores. Data moves between devices by JAX's collectives and lax.ppermute only.
A program may use at most 128 MiB of HBM per device.

```python
import math
import jax
import jax.numpy as jnp
from jax import lax

D = 5120
HEADS = 32
HD = 128
FT = 128
SLOTS = 4
LEVELS = 32
TOK_DEV = 128
TOKENS = 2048
CFRAMES = 16
HIST_FRAMES = 64
N_CTX = 16


def history_layout(key):
    return jax.random.permutation(key, HIST_FRAMES)


def draw_frame_home(key, part):
    placed = history_layout(key)
    return placed.astype(jnp.int32)


def draw_hist_list(key, part):
    placed = history_layout(key)
    key = jax.random.fold_in(key, 5)
    owner_key, slot_key = jax.random.split(key)
    owner_order = jax.vmap(lambda single: jax.random.permutation(single, N_CTX))(jax.random.split(owner_key, N_CTX))
    local_slot = jax.random.randint(slot_key, (N_CTX, N_CTX), 0, SLOTS)
    slot_index = owner_order * SLOTS + local_slot
    frame_of_slot = jnp.zeros((HIST_FRAMES,), jnp.int32).at[placed].set(jnp.arange(HIST_FRAMES, dtype=jnp.int32))
    return frame_of_slot[slot_index].astype(jnp.int32)


def draw_list_count(key, part):
    key = jax.random.fold_in(key, 7)
    count_key, full_key = jax.random.split(key)
    counts = jax.random.randint(count_key, (N_CTX,), N_CTX // 2, N_CTX + 1)
    full_reader = jax.random.randint(full_key, (), 0, N_CTX)
    return counts.at[full_reader].set(N_CTX).astype(jnp.int32)


def draw_noise_levels(key, part):
    key = jax.random.fold_in(key, 11)
    start_key, top_key, first_key, second_key = jax.random.split(key, 4)
    start_level = jax.random.randint(start_key, (CFRAMES,), LEVELS // 2, LEVELS)
    top_frame = jax.random.randint(top_key, (), 0, CFRAMES)
    start_level = start_level.at[top_frame].set(LEVELS - 1)
    first_drop = jax.random.randint(first_key, (CFRAMES,), 1, LEVELS // 4 + 1)
    second_drop = jax.random.randint(second_key, (CFRAMES,), 1, LEVELS // 4 + 1)
    middle_level = start_level - first_drop
    return jnp.stack([start_level, middle_level, middle_level - second_drop]).astype(jnp.int32)


def draw_hist_keys(key, part):
    key = jax.random.fold_in(key, 13)
    base_key = jax.random.fold_in(key, 0)
    shape_all = (HIST_FRAMES, FT, HEADS * HD)
    base_value = jnp.clip(jax.random.normal(base_key, shape_all, jnp.float32), -6.0, 6.0)
    return base_value.astype(jnp.bfloat16)


def shard_levels(own_key, extent, cuts, low, high):
    def one(dim, blocks):
        draws = jax.random.uniform(jax.random.fold_in(jax.random.fold_in(own_key, 6), dim), (blocks,), jnp.float32, low / len(cuts), high / len(cuts))
        return jnp.repeat(jnp.exp(draws), extent[dim] // blocks).reshape((-1,) + (1,) * (len(extent) - dim - 1))

    level = one(*cuts[0])
    for cut in cuts[1:]:
        level = level * one(*cut)
    return level


def centred(rng, dims, width, limit, shards=(), kind=jnp.bfloat16):
    entries = width * jax.random.normal(rng, dims, jnp.float32)
    if shards:
        entries = entries * shard_levels(rng, dims, shards, -0.22, 0.18)
    return jnp.clip(entries, -limit, limit).astype(kind)


def setup_inputs(seed: int = 0) -> dict:
    splits = jax.random.split(jax.random.key(seed), 13)
    return {
        "latent": centred(splits[0], (TOKENS, D), 0.5, 2.5, ((0, 16), (1, 16))),
        "noise_levels": draw_noise_levels(jax.random.fold_in(splits[12], 71), 0),
        "mod_table": centred(splits[2], (LEVELS, 2, D), 0.3, 2.5, (), jnp.float32),
        "w_query": centred(splits[3], (D, HEADS * HD), D ** -0.5, 0.078125, ((1, 16),)),
        "w_key": centred(splits[4], (D, HEADS * HD), D ** -0.5, 0.078125, ((1, 16),)),
        "w_value": centred(splits[5], (D, HEADS * HD), D ** -0.5, 0.078125, ((1, 16),)),
        "w_out": centred(splits[6], (HEADS * HD, D), (HEADS * HD) ** -0.5, 0.09375, ((0, 16),)),
        "hist_keys": draw_hist_keys(jax.random.fold_in(splits[12], 71), 0),
        "hist_values": centred(splits[8], (HIST_FRAMES, FT, HEADS * HD), 1.0, 6.0, ((0, 16), (2, 16))),
        "frame_home": draw_frame_home(jax.random.fold_in(splits[12], 71), 0),
        "hist_list": draw_hist_list(jax.random.fold_in(splits[12], 71), 0),
        "list_count": draw_list_count(jax.random.fold_in(splits[12], 71), 0),
    }


def reference(latent, noise_levels, mod_table, w_query, w_key, w_value, w_out, hist_keys, hist_values, frame_home, hist_list, list_count):
    noise_sigma = (noise_levels.astype(jnp.float32) + 1.0) / LEVELS
    hist_slots = frame_home[hist_list]
    score_scale = 1.0 / math.sqrt(HD)
    key_frame = jnp.arange(TOKENS, dtype=jnp.int32) // FT
    latent_now = latent
    velocity_list = []
    for denoise_step in range(2):
        modulation = mod_table[noise_levels[denoise_step]]
        wide_rows = latent_now.astype(jnp.float32).reshape(CFRAMES, FT, D)
        meansq = lax.optimization_barrier(jnp.mean(wide_rows * wide_rows, axis=-1, keepdims=True))
        normed = wide_rows * lax.rsqrt(meansq + 1e-06) * (1.0 + modulation[:, 1][:, None, :]) + modulation[:, 0][:, None, :]
        normed = normed.astype(jnp.bfloat16).reshape(TOKENS, D)
        query_rows = jnp.dot(normed, w_query, preferred_element_type=jnp.float32).astype(jnp.bfloat16)
        key_rows = jnp.dot(normed, w_key, preferred_element_type=jnp.float32).astype(jnp.bfloat16)
        value_rows = jnp.dot(normed, w_value, preferred_element_type=jnp.float32).astype(jnp.bfloat16)

        def block_attention(block_index):
            block_query = lax.dynamic_slice_in_dim(query_rows, block_index * TOK_DEV, TOK_DEV, 0)
            block_query = block_query.reshape(TOK_DEV, HEADS, HD).astype(jnp.float32)
            slot_row = hist_slots[block_index]
            past_keys = hist_keys[slot_row].reshape(N_CTX * FT, HEADS, HD)
            past_values = hist_values[slot_row].reshape(N_CTX * FT, HEADS, HD)
            all_keys = jnp.concatenate([key_rows.reshape(TOKENS, HEADS, HD), past_keys], axis=0).astype(jnp.float32)
            all_values = jnp.concatenate([value_rows.reshape(TOKENS, HEADS, HD), past_values], axis=0).astype(jnp.float32)
            query_frame = (block_index * TOK_DEV + jnp.arange(TOK_DEV, dtype=jnp.int32)) // FT
            group_mask = query_frame[:, None] >= key_frame[None, :]
            past_live = jnp.arange(N_CTX * FT, dtype=jnp.int32) // FT < list_count[block_index]
            past_mask = jnp.broadcast_to(past_live[None, :], (TOK_DEV, N_CTX * FT))
            key_mask = jnp.concatenate([group_mask, past_mask], axis=1)
            scores = jnp.einsum('qhd,khd->hqk', block_query, all_keys) * score_scale
            scores = jnp.where(key_mask[None], scores, -1e+30)
            row_max = lax.optimization_barrier(jnp.max(scores, axis=-1, keepdims=True))
            weights = jnp.where(key_mask[None], jnp.exp(scores - row_max), 0.0)
            weight_sum = lax.optimization_barrier(jnp.sum(weights, axis=-1))
            accumulated = jnp.einsum('hqk,khd->hqd', weights.astype(jnp.bfloat16).astype(jnp.float32), all_values)
            result = accumulated / weight_sum[..., None]
            return jnp.transpose(result, (1, 0, 2)).reshape(TOK_DEV, HEADS * HD).astype(jnp.bfloat16)
        attended = lax.map(block_attention, jnp.arange(N_CTX, dtype=jnp.int32)).reshape(TOKENS, HEADS * HD)
        velocity = jnp.dot(attended, w_out, preferred_element_type=jnp.float32).astype(jnp.bfloat16)
        step_size = jnp.repeat(noise_sigma[denoise_step + 1] - noise_sigma[denoise_step], FT)[:, None]
        latent_now = (latent_now.astype(jnp.float32) + step_size * velocity.astype(jnp.float32)).astype(jnp.bfloat16)
        velocity_list.append(velocity)
    return (latent_now, jnp.stack(velocity_list))
```

```python
import math

import jax
import jax.numpy as jnp
from jax import lax
from jax.sharding import Mesh, PartitionSpec as P

HD = 128
CTX = ("yl", "x", "core")
CHIPS = ("yl", "x")
TP = ("yh", "z")


def per_device(
    latent,
    noise_levels,
    mod_table,
    w_query,
    w_key,
    w_value,
    w_out,
    hist_keys,
    hist_values,
    frame_home,
    hist_list,
    list_count,
):
    tok, width = latent.shape
    level_count, _, full = mod_table.shape
    heads = w_query.shape[1] // HD
    hw = heads * HD
    n_ctx = lax.axis_size(CTX)
    n_chip = lax.axis_size(CHIPS)
    n_tp = lax.axis_size(TP)
    n_z = lax.axis_size("z")
    core = lax.axis_index("core")
    chip = lax.axis_index(CHIPS)
    tp_id = lax.axis_index(TP)
    rows = tok // n_tp
    f32, bf16 = jnp.float32, jnp.bfloat16
    scale = 1.0 / math.sqrt(HD)
    swap = [(0, 1), (1, 0)]

    sigma = (noise_levels[:, 0].astype(f32) + 1.0) / level_count
    steps = sigma[1:] - sigma[:-1]

    slot_per_owner, past_len, _ = hist_keys.shape
    wanted = frame_home[hist_list[0]]
    matched = (wanted // slot_per_owner)[:, None] == jnp.arange(n_ctx, dtype=jnp.int32)[None, :]
    request = jnp.sum(jnp.where(matched, (wanted % slot_per_owner)[:, None], 0), axis=0)
    in_list = jnp.arange(n_ctx, dtype=jnp.int32) < list_count[0]
    valid_owner = jnp.any(matched & in_list[:, None], axis=0)
    picked = lax.all_to_all(request[:, None], CTX, split_axis=0, concat_axis=0, tiled=True)[:, 0]
    hist = jnp.concatenate([hist_keys, hist_values], axis=2)
    past = lax.all_to_all(hist[picked], CTX, split_axis=0, concat_axis=0, tiled=True)

    own = latent.T
    other = lax.ppermute(own, "yh", swap)
    is_hi = lax.axis_index("yh") == 1
    pair = jnp.stack([jnp.where(is_hi, other, own), jnp.where(is_hi, own, other)])
    gathered = lax.all_gather(pair, "z", axis=0)
    full_t = jnp.transpose(gathered, (1, 0, 2, 3)).reshape(full, tok)
    full_rows = full_t.T

    def norm(x, step):
        mod = mod_table[noise_levels[step, 0]]
        wide = x.astype(f32)
        meansq = jnp.mean(wide * wide, axis=-1, keepdims=True)
        out = wide * lax.rsqrt(meansq + 1e-06) * (1.0 + mod[1][None]) + mod[0][None]
        return out.astype(bf16)

    own_rows = lax.dynamic_slice_in_dim(full_rows, tp_id * rows, rows, 0)
    normed = norm(full_rows, 0)

    chips = jnp.arange(n_chip, dtype=jnp.int32)
    seen_own = chips <= chip
    seen_other = (chips < chip) | ((chips == chip) & (core == 1))
    live = jnp.concatenate([seen_own, seen_other, valid_owner])
    live = jnp.repeat(live, tok)[None, None, :]

    def attend(normed):
        k = jnp.dot(normed, w_key, preferred_element_type=f32).astype(bf16)
        v = jnp.dot(normed, w_value, preferred_element_type=f32).astype(bf16)
        kv = jnp.concatenate([k, v], axis=1)
        near = lax.all_to_all(
            jnp.broadcast_to(kv[None], (n_chip, tok, 2 * hw)), CHIPS, split_axis=0, concat_axis=0, tiled=True
        )
        far = lax.ppermute(near, "core", swap)
        q = jnp.dot(normed, w_query, preferred_element_type=f32).astype(bf16).reshape(tok, heads, HD)
        every = jnp.concatenate([near, far, past], axis=0).reshape(-1, 2 * hw)
        keys = every[:, :hw].reshape(-1, heads, HD)
        values = every[:, hw:].reshape(-1, heads, HD)
        scores = jnp.einsum("qhd,khd->hqk", q, keys, preferred_element_type=f32) * scale
        scores = jnp.where(live, scores, -1e30)
        top = jnp.max(scores, axis=-1, keepdims=True)
        weights = jnp.where(live, jnp.exp(scores - top), 0.0)
        total = jnp.sum(weights, axis=-1)
        acc = jnp.einsum("hqk,khd->hqd", weights.astype(bf16), values, preferred_element_type=f32)
        out = jnp.transpose(acc / total[..., None], (1, 0, 2)).reshape(tok, hw).astype(bf16)
        return jnp.dot(out, w_out, preferred_element_type=f32).astype(bf16)

    part = attend(normed).reshape(n_tp, rows, full)
    got = lax.all_to_all(part, TP, split_axis=0, concat_axis=0, tiled=True)
    v0_rows = jnp.sum(got.astype(f32), axis=0).astype(bf16)
    x1_rows = (own_rows.astype(f32) + steps[0] * v0_rows.astype(f32)).astype(bf16)
    normed_rows = norm(x1_rows, 1)
    pad = -width % 128
    v0_send = jnp.pad(jnp.transpose(v0_rows.reshape(rows, n_tp, width), (1, 0, 2)), ((0, 0), (0, 0), (0, pad)))
    send = jnp.concatenate([jnp.broadcast_to(normed_rows[None], (n_tp, rows, full)), v0_send], axis=2)
    got = lax.all_to_all(send, TP, split_axis=0, concat_axis=0, tiled=True)
    normed = got[:, :, :full].reshape(tok, full)
    v0 = got[:, :, full : full + width].reshape(tok, width)
    x1 = (latent.astype(f32) + steps[0] * v0.astype(f32)).astype(bf16)

    part = attend(normed)
    part = jnp.transpose(part.reshape(tok, n_tp, width), (1, 2, 0))
    got = lax.all_to_all(part, TP, split_axis=0, concat_axis=0, tiled=True)
    v1 = jnp.sum(got.astype(f32), axis=0).astype(bf16).T
    x2 = (x1.astype(f32) + steps[1] * v1.astype(f32)).astype(bf16)
    return x2, jnp.stack([v0, v1])


def solution(mesh):
    fine = Mesh(mesh.devices.reshape(2, 4, 2, 2, 8), ("yl", "x", "core", "yh", "z"))
    return jax.shard_map(
        per_device,
        mesh=fine,
        in_specs=(
            P(CTX, TP),
            P(None, CTX),
            P(),
            P(None, TP),
            P(None, TP),
            P(None, TP),
            P(TP, None),
            P(CTX, None, TP),
            P(CTX, None, TP),
            P(),
            P(CTX, None),
            P(CTX),
        ),
        out_specs=(P(CTX, TP), P(None, CTX, TP)),
        check_vma=False,
    )
```

```python
import math

import jax
import jax.numpy as jnp
from jax import lax
from jax.sharding import Mesh, PartitionSpec as P

HD = 128
CTX = ("yl", "x", "core")
CHIPS = ("yl", "x")
TP = ("yh", "z")


def per_device(
    latent,
    noise_levels,
    mod_table,
    w_query,
    w_key,
    w_value,
    w_out,
    hist_keys,
    hist_values,
    frame_home,
    hist_list,
    list_count,
):
    tok, width = latent.shape
    level_count, _, full = mod_table.shape
    heads = w_query.shape[1] // HD
    hw = heads * HD
    n_ctx = lax.axis_size(CTX)
    n_chip = lax.axis_size(CHIPS)
    n_z = lax.axis_size("z")
    n_yh = lax.axis_size("yh")
    yh = lax.axis_index("yh")
    core = lax.axis_index("core")
    chip = lax.axis_index(CHIPS)
    z = lax.axis_index("z")
    rows = tok // n_z
    f32, bf16 = jnp.float32, jnp.bfloat16
    scale = 1.0 / math.sqrt(HD)
    swap = [(0, 1), (1, 0)]

    sigma = (noise_levels[:, 0].astype(f32) + 1.0) / level_count
    steps = sigma[1:] - sigma[:-1]

    slot_per_owner, past_len, _ = hist_keys.shape
    wanted = frame_home[hist_list[0]]
    matched = (wanted // slot_per_owner)[:, None] == jnp.arange(n_ctx, dtype=jnp.int32)[None, :]
    request = jnp.sum(jnp.where(matched, (wanted % slot_per_owner)[:, None], 0), axis=0)
    in_list = jnp.arange(n_ctx, dtype=jnp.int32) < list_count[0]
    valid_owner = jnp.any(matched & in_list[:, None], axis=0)
    picked = lax.all_to_all(request[:, None], CTX, split_axis=0, concat_axis=0, tiled=True)[:, 0]
    hist = jnp.concatenate([hist_keys, hist_values], axis=2)
    past = lax.all_to_all(hist[picked], CTX, split_axis=0, concat_axis=0, tiled=True)

    own = latent.T
    other = lax.ppermute(own, "yh", swap)
    pair = jnp.stack([jnp.where(yh == 1, other, own), jnp.where(yh == 1, own, other)])
    gathered = lax.all_gather(pair, "z", axis=0)
    gathered, past = lax.optimization_barrier((gathered, past))
    full_t = jnp.transpose(gathered, (1, 0, 2, 3)).reshape(full, tok)
    full_rows = full_t.T

    def norm(x, step):
        mod = mod_table[noise_levels[step, 0]]
        wide = x.astype(f32)
        meansq = jnp.mean(wide * wide, axis=-1, keepdims=True)
        out = wide * lax.rsqrt(meansq + 1e-06) * (1.0 + mod[1][None]) + mod[0][None]
        return out.astype(bf16)

    own_rows = lax.dynamic_slice_in_dim(full_rows, z * rows, rows, 0)
    normed = norm(full_rows, 0)

    chips = jnp.arange(n_chip, dtype=jnp.int32)
    seen_own = chips <= chip
    seen_other = (chips < chip) | ((chips == chip) & (core == 1))
    live = jnp.concatenate([seen_own, seen_other, valid_owner])
    live = jnp.repeat(live, tok)[None, None, :]

    def attend(normed):
        k = jnp.dot(normed, w_key, preferred_element_type=f32).astype(bf16)
        v = jnp.dot(normed, w_value, preferred_element_type=f32).astype(bf16)
        kv = jnp.concatenate([k, v], axis=1)
        near = lax.all_to_all(
            jnp.broadcast_to(kv[None], (n_chip, tok, 2 * hw)), CHIPS, split_axis=0, concat_axis=0, tiled=True
        )
        far = lax.ppermute(near, "core", swap)
        q = jnp.dot(normed, w_query, preferred_element_type=f32).astype(bf16).reshape(tok, heads, HD)
        every = jnp.concatenate([near, far, past], axis=0).reshape(-1, 2 * hw)
        keys = every[:, :hw].reshape(-1, heads, HD)
        values = every[:, hw:].reshape(-1, heads, HD)
        scores = jnp.einsum("qhd,khd->hqk", q, keys, preferred_element_type=f32) * scale
        scores = jnp.where(live, scores, -1e30)
        top = jnp.max(scores, axis=-1, keepdims=True)
        weights = jnp.where(live, jnp.exp(scores - top), 0.0)
        total = jnp.sum(weights, axis=-1)
        acc = jnp.einsum("hqk,khd->hqd", weights.astype(bf16), values, preferred_element_type=f32)
        out = jnp.transpose(acc / total[..., None], (1, 0, 2)).reshape(tok, hw).astype(bf16)
        return jnp.dot(out, w_out, preferred_element_type=f32).astype(bf16)

    def to_z(blocks):
        return lax.all_to_all(blocks, "z", split_axis=0, concat_axis=0, tiled=True)

    part = attend(normed).reshape(n_z, rows, full)
    half = jnp.sum(to_z(part).astype(f32), axis=0).astype(bf16)
    rest = lax.ppermute(half, "yh", swap)
    v0_rows = (half.astype(f32) + rest.astype(f32)).astype(bf16)
    x1_rows = (own_rows.astype(f32) + steps[0] * v0_rows.astype(f32)).astype(bf16)
    normed_rows = norm(x1_rows, 1)
    pad = -width % 128
    mine = lax.dynamic_index_in_dim(v0_rows.reshape(rows, n_yh, n_z, width), yh, 1, keepdims=False)
    v0_send = jnp.pad(jnp.transpose(mine, (1, 0, 2)), ((0, 0), (0, 0), (0, pad)))
    got = to_z(jnp.concatenate([jnp.broadcast_to(normed_rows[None], (n_z, rows, full)), v0_send], axis=2))
    normed = got[:, :, :full].reshape(tok, full)
    v0 = got[:, :, full : full + width].reshape(tok, width)
    x1 = (latent.astype(f32) + steps[0] * v0.astype(f32)).astype(bf16)

    part = jnp.transpose(attend(normed).reshape(tok, n_yh, n_z, width), (2, 1, 3, 0))
    halves = jnp.sum(to_z(part).astype(f32), axis=0).astype(bf16)
    keep = jnp.where(yh == 1, halves[1], halves[0])
    give = jnp.where(yh == 1, halves[0], halves[1])
    rest = lax.ppermute(give, "yh", swap)
    v1 = (keep.astype(f32) + rest.astype(f32)).astype(bf16).T
    x2 = (x1.astype(f32) + steps[1] * v1.astype(f32)).astype(bf16)
    return x2, jnp.stack([v0, v1])


def solution(mesh):
    fine = Mesh(mesh.devices.reshape(2, 4, 2, 2, 8), ("yl", "x", "core", "yh", "z"))
    return jax.shard_map(
        per_device,
        mesh=fine,
        in_specs=(
            P(CTX, TP),
            P(None, CTX),
            P(),
            P(None, TP),
            P(None, TP),
            P(None, TP),
            P(TP, None),
            P(CTX, None, TP),
            P(CTX, None, TP),
            P(),
            P(CTX, None),
            P(CTX),
        ),
        out_specs=(P(CTX, TP), P(None, CTX, TP)),
        check_vma=False,
    )
```

```python
import functools
import math

import jax
import jax.numpy as jnp
from jax import lax
from jax.experimental import pallas as pl
from jax.experimental.pallas import tpu as pltpu
from jax.sharding import Mesh, PartitionSpec as P

HD = 128
CTX = ("yl", "x", "core")
CHIPS = ("yl", "x")
TP = ("yh", "z")
F32, BF16 = jnp.float32, jnp.bfloat16
LOW = -1e30
SWAP = [(0, 1), (1, 0)]


def block_scores(q, live_ref, base, keys, score_scr, scale):
    top = None
    for j, key in enumerate(keys):
        s = lax.dot_general(q, key, (((1,), (1,)), ((), ())), preferred_element_type=F32) * scale
        s = s + jnp.where(live_ref[base + j] > 0, 0.0, LOW)
        score_scr[:, j * HD : (j + 1) * HD] = s
        top = s if top is None else jnp.maximum(top, s)
    return jnp.max(top, axis=1, keepdims=True)


def weigh(score_scr, weight_scr, top, blocks):
    total = None
    for j in range(blocks):
        w = jnp.exp(score_scr[:, j * HD : (j + 1) * HD] - top)
        weight_scr[:, j * HD : (j + 1) * HD] = w.astype(BF16)
        total = w if total is None else total + w
    return jnp.sum(total, axis=1, keepdims=True)


def past_kernel(heads, scale, live_ref, q_ref, past_ref, top_ref, total_ref, acc_ref, score_scr, weight_scr):
    blocks, past_len, _ = past_ref.shape
    for h in range(heads):
        cut = slice(h * HD, (h + 1) * HD)
        v_cut = slice((heads + h) * HD, (heads + h + 1) * HD)
        keys = [past_ref[j, :, cut] for j in range(blocks)]
        top = block_scores(q_ref[:, cut], live_ref, 0, keys, score_scr, scale)
        total = weigh(score_scr, weight_scr, top, blocks)
        values = past_ref[:, :, v_cut].reshape(blocks * past_len, HD)
        acc_ref[:, cut] = jnp.dot(weight_scr[...], values, preferred_element_type=F32)
        top_ref[:, cut] = jnp.broadcast_to(top, (q_ref.shape[0], HD))
        total_ref[:, cut] = jnp.broadcast_to(total, (q_ref.shape[0], HD))


def group_kernel(
    heads, scale, by_token, live_ref, place_ref, q_ref, near_ref, far_ref, top_ref, total_ref, acc_ref, w_ref,
    out_ref, score_scr, weight_scr, att_scr,
):
    chips, tok, _ = near_ref.shape
    z = place_ref[0]
    n_z = out_ref.shape[0]
    rows = tok // n_z
    for h in range(heads):
        cut = slice(h * HD, (h + 1) * HD)
        v_cut = slice((heads + h) * HD, (heads + h + 1) * HD)
        keys = [near_ref[j, :, cut] for j in range(chips)] + [far_ref[j, :, cut] for j in range(chips)]
        top = block_scores(q_ref[:, cut], live_ref, 0, keys, score_scr, scale)
        past_top = top_ref[:, cut]
        new_top = jnp.maximum(past_top, top)
        total = weigh(score_scr, weight_scr, new_top, 2 * chips)
        shrink = jnp.exp(past_top - new_top)
        acc = acc_ref[:, cut] * shrink
        half = chips * tok
        acc = acc + jnp.dot(
            weight_scr[:, :half], near_ref[:, :, v_cut].reshape(half, HD), preferred_element_type=F32
        )
        acc = acc + jnp.dot(
            weight_scr[:, half:], far_ref[:, :, v_cut].reshape(half, HD), preferred_element_type=F32
        )
        att = (acc / (total_ref[:, cut] * shrink + total)).astype(BF16)
        if by_token:
            att_scr[:, cut] = att
        else:
            for k in range(n_z):
                row = pl.multiple_of(lax.rem(z + k, n_z) * rows, rows)
                att_scr[pl.ds(row, rows), cut] = att[k * rows : (k + 1) * rows]
    full = w_ref.shape[1]
    width = out_ref.shape[2] if not by_token else full // 16
    step = 2 * width
    for c in range(full // step):
        o = jnp.dot(att_scr[...], w_ref[:, c * step : (c + 1) * step], preferred_element_type=F32)
        if by_token:
            o = o.astype(BF16)
            for r in range(n_z):
                out_ref[lax.rem(r + n_z - z, n_z), :, c * step : (c + 1) * step] = o[r * rows : (r + 1) * rows]
        else:
            o = o.T.astype(BF16)
            for half in range(2):
                block = 2 * c + half
                out_ref[lax.rem(block % n_z + n_z - z, n_z), block // n_z] = o[half * width : (half + 1) * width]


def per_device(
    latent,
    noise_levels,
    mod_table,
    w_query,
    w_key,
    w_value,
    w_out,
    hist_keys,
    hist_values,
    frame_home,
    hist_list,
    list_count,
):
    tok, width = latent.shape
    level_count, _, full = mod_table.shape
    heads = w_query.shape[1] // HD
    hw = heads * HD
    n_ctx = lax.axis_size(CTX)
    n_chip = lax.axis_size(CHIPS)
    n_z = lax.axis_size("z")
    n_yh = lax.axis_size("yh")
    yh = lax.axis_index("yh")
    core = lax.axis_index("core")
    chip = lax.axis_index(CHIPS)
    z = lax.axis_index("z")
    rows = tok // n_z
    scale = 1.0 / math.sqrt(HD)
    down = [(i, (i - 1) % n_z) for i in range(n_z)]
    up = [(i, (i + 1) % n_z) for i in range(n_z)]

    def ring_gather(*chains):
        got = [{0: c} for c in chains]
        for k in range(1, n_z // 2 + 1):
            for g in got:
                g[k] = lax.ppermute(g[k - 1], "z", down)
                if 2 * k < n_z:
                    g[-k] = lax.ppermute(g[1 - k], "z", up)
        return [[g[k] if 2 * k <= n_z else g[k - n_z] for k in range(n_z)] for g in got]

    def ring_sum(parts):
        low = parts[n_z // 2]
        high = parts[n_z // 2 - 1]
        for k in range(n_z // 2, 0, -1):
            low = lax.ppermute(low, "z", down)
            if k > 1:
                low = (low.astype(F32) + parts[n_z - k + 1].astype(F32)).astype(BF16)
            if 2 * k < n_z:
                high = lax.ppermute(high, "z", up)
                if k > 1:
                    high = (high.astype(F32) + parts[k - 1].astype(F32)).astype(BF16)
        return parts[0].astype(F32) + low.astype(F32) + high.astype(F32)

    sigma = (noise_levels[:, 0].astype(F32) + 1.0) / level_count
    steps = sigma[1:] - sigma[:-1]

    slot_per_owner, past_len, _ = hist_keys.shape
    wanted = frame_home[hist_list[0]]
    matched = (wanted // slot_per_owner)[:, None] == jnp.arange(n_ctx, dtype=jnp.int32)[None, :]
    request = jnp.sum(jnp.where(matched, (wanted % slot_per_owner)[:, None], 0), axis=0)
    in_list = jnp.arange(n_ctx, dtype=jnp.int32) < list_count[0]
    valid_owner = jnp.any(matched & in_list[:, None], axis=0)
    picked = lax.all_to_all(request[:, None], CTX, split_axis=0, concat_axis=0, tiled=True)[:, 0]
    hist = jnp.concatenate([hist_keys, hist_values], axis=2)
    past = lax.all_to_all(hist[picked], CTX, split_axis=0, concat_axis=0, tiled=True)

    own = latent.T
    other = lax.ppermute(own, "yh", SWAP)
    got_own, got_other = ring_gather(own, other)
    near_z = jnp.stack([jnp.stack(got_own), jnp.stack(got_other)])
    near_z = jnp.where(yh == 1, near_z[::-1], near_z)
    twice = jnp.concatenate([near_z, near_z], axis=1)
    full_t = lax.dynamic_slice_in_dim(twice, n_z - z, n_z, 1).reshape(full, tok)
    full_rows = full_t.T

    def norm(x, step):
        mod = mod_table[noise_levels[step, 0]]
        wide = x.astype(F32)
        meansq = jnp.mean(wide * wide, axis=-1, keepdims=True)
        out = wide * lax.rsqrt(meansq + 1e-06) * (1.0 + mod[1][None]) + mod[0][None]
        return out.astype(BF16)

    own_rows = lax.dynamic_slice_in_dim(full_rows, z * rows, rows, 0)
    normed = norm(full_rows, 0)

    chips = jnp.arange(n_chip, dtype=jnp.int32)
    seen_own = chips <= chip
    seen_other = (chips < chip) | ((chips == chip) & (core == 1))
    group_live = jnp.concatenate([seen_own, seen_other]).astype(jnp.int32)
    past_live = valid_owner.astype(jnp.int32)
    place = z.astype(jnp.int32).reshape(1)

    smem = pl.BlockSpec(memory_space=pltpu.SMEM)
    vmem = pl.BlockSpec(memory_space=pltpu.VMEM)
    limit = pltpu.CompilerParams(vmem_limit_bytes=24 * 2**20)

    def attend(normed, past, by_token):
        k = jnp.dot(normed, w_key, preferred_element_type=F32).astype(BF16)
        v = jnp.dot(normed, w_value, preferred_element_type=F32).astype(BF16)
        kv = jnp.concatenate([k, v], axis=1)
        kv, past = lax.optimization_barrier((kv, past))
        near = lax.all_to_all(
            jnp.broadcast_to(kv[None], (n_chip, tok, 2 * hw)), CHIPS, split_axis=0, concat_axis=0, tiled=True
        )
        far = lax.ppermute(near, "core", SWAP)
        q = jnp.dot(normed, w_query, preferred_element_type=F32).astype(BF16)
        stat = jax.ShapeDtypeStruct((tok, hw), F32)
        top, total, acc = pl.pallas_call(
            functools.partial(past_kernel, heads, scale),
            out_shape=[stat, stat, stat],
            in_specs=[smem, vmem, vmem],
            out_specs=[vmem, vmem, vmem],
            scratch_shapes=[
                pltpu.VMEM((tok, n_ctx * past_len), F32),
                pltpu.VMEM((tok, n_ctx * past_len), BF16),
            ],
            compiler_params=limit,
            cost_estimate=pl.CostEstimate(
                flops=4 * tok * n_ctx * past_len * hw,
                bytes_accessed=n_ctx * past_len * hw * 4,
                transcendentals=tok * n_ctx * past_len * heads,
            ),
        )(past_live, q, past)
        shape = (n_z, rows, full) if by_token else (n_z, n_yh, width, tok)
        return pl.pallas_call(
            functools.partial(group_kernel, heads, scale, by_token),
            out_shape=jax.ShapeDtypeStruct(shape, BF16),
            in_specs=[smem, smem] + [vmem] * 7,
            out_specs=vmem,
            scratch_shapes=[
                pltpu.VMEM((tok, 2 * n_chip * tok), F32),
                pltpu.VMEM((tok, 2 * n_chip * tok), BF16),
                pltpu.VMEM((tok, hw), BF16),
            ],
            compiler_params=limit,
            cost_estimate=pl.CostEstimate(
                flops=4 * tok * 2 * n_chip * tok * hw + 2 * tok * hw * full,
                bytes_accessed=2 * n_chip * tok * hw * 4 + hw * full * 2 + tok * full * 2,
                transcendentals=tok * 2 * n_chip * tok * heads,
            ),
        )(group_live, place, q, near, far, top, total, acc, w_out)

    part = attend(normed, past, True)
    half = ring_sum([part[k] for k in range(n_z)]).astype(BF16)
    rest = lax.ppermute(half, "yh", SWAP)
    v0_rows = (half.astype(F32) + rest.astype(F32)).astype(BF16)
    x1_rows = (own_rows.astype(F32) + steps[0] * v0_rows.astype(F32)).astype(BF16)
    normed_rows = norm(x1_rows, 1)
    first, second = ring_gather(normed_rows[: rows // 2], normed_rows[rows // 2 :])
    normed = jnp.concatenate([r for pair in zip(first, second) for r in pair], axis=0)
    mine = lax.dynamic_index_in_dim(v0_rows.reshape(rows, n_yh, n_z, width), yh, 1, keepdims=False)
    v0 = lax.all_to_all(jnp.transpose(mine, (1, 0, 2)), "z", split_axis=0, concat_axis=0, tiled=True)
    v0 = v0.reshape(tok, width)
    x1 = (latent.astype(F32) + steps[0] * v0.astype(F32)).astype(BF16)

    part = attend(normed, past, False)
    halves = ring_sum([part[k] for k in range(n_z)]).astype(BF16)
    keep = jnp.where(yh == 1, halves[1], halves[0])
    give = jnp.where(yh == 1, halves[0], halves[1])
    rest = lax.ppermute(give, "yh", SWAP)
    v1 = (keep.astype(F32) + rest.astype(F32)).astype(BF16).T
    x2 = (x1.astype(F32) + steps[1] * v1.astype(F32)).astype(BF16)
    return x2, jnp.stack([v0, v1])


def solution(mesh):
    fine = Mesh(mesh.devices.reshape(2, 4, 2, 2, 8), ("yl", "x", "core", "yh", "z"))
    return jax.shard_map(
        per_device,
        mesh=fine,
        in_specs=(
            P(CTX, TP),
            P(None, CTX),
            P(),
            P(None, TP),
            P(None, TP),
            P(None, TP),
            P(TP, None),
            P(CTX, None, TP),
            P(CTX, None, TP),
            P(),
            P(CTX, None),
            P(CTX),
        ),
        out_specs=(P(CTX, TP), P(None, CTX, TP)),
        check_vma=False,
    )
```

```python
import functools
import math

import jax
import jax.numpy as jnp
from jax import lax
from jax.experimental import pallas as pl
from jax.experimental.pallas import tpu as pltpu
from jax.sharding import Mesh, PartitionSpec as P

HD = 128
CTX = ("yl", "x", "core")
CHIPS = ("yl", "x")
TP = ("yh", "z")
F32, BF16 = jnp.float32, jnp.bfloat16
LOW = -1e30
SWAP = [(0, 1), (1, 0)]


def block_scores(q, live_ref, base, keys, score_scr, scale):
    top = None
    for j, key in enumerate(keys):
        s = lax.dot_general(q, key, (((1,), (1,)), ((), ())), preferred_element_type=F32) * scale
        s = s + jnp.where(live_ref[base + j] > 0, 0.0, LOW)
        score_scr[:, j * HD : (j + 1) * HD] = s
        top = s if top is None else jnp.maximum(top, s)
    return jnp.max(top, axis=1, keepdims=True)


def weigh(score_scr, weight_scr, top, blocks):
    total = None
    for j in range(blocks):
        w = jnp.exp(score_scr[:, j * HD : (j + 1) * HD] - top)
        weight_scr[:, j * HD : (j + 1) * HD] = w.astype(BF16)
        total = w if total is None else total + w
    return jnp.sum(total, axis=1, keepdims=True)


def past_kernel(heads, scale, live_ref, q_ref, past_ref, top_ref, total_ref, acc_ref, score_scr, weight_scr):
    blocks, past_len, _ = past_ref.shape
    for h in range(heads):
        cut = slice(h * HD, (h + 1) * HD)
        v_cut = slice((heads + h) * HD, (heads + h + 1) * HD)
        keys = [past_ref[j, :, cut] for j in range(blocks)]
        top = block_scores(q_ref[:, cut], live_ref, 0, keys, score_scr, scale)
        total = weigh(score_scr, weight_scr, top, blocks)
        values = past_ref[:, :, v_cut].reshape(blocks * past_len, HD)
        acc_ref[:, cut] = jnp.dot(weight_scr[...], values, preferred_element_type=F32)
        top_ref[:, cut] = jnp.broadcast_to(top, (q_ref.shape[0], HD))
        total_ref[:, cut] = jnp.broadcast_to(total, (q_ref.shape[0], HD))


def group_kernel(
    heads, scale, by_token, live_ref, place_ref, q_ref, near_ref, far_ref, top_ref, total_ref, acc_ref, w_ref,
    out_ref, score_scr, weight_scr, att_scr,
):
    chips, tok, _ = near_ref.shape
    z = place_ref[0]
    n_z = out_ref.shape[0]
    rows = tok // n_z
    for h in range(heads):
        cut = slice(h * HD, (h + 1) * HD)
        v_cut = slice((heads + h) * HD, (heads + h + 1) * HD)
        keys = [near_ref[j, :, cut] for j in range(chips)] + [far_ref[j, :, cut] for j in range(chips)]
        top = block_scores(q_ref[:, cut], live_ref, 0, keys, score_scr, scale)
        past_top = top_ref[:, cut]
        new_top = jnp.maximum(past_top, top)
        total = weigh(score_scr, weight_scr, new_top, 2 * chips)
        shrink = jnp.exp(past_top - new_top)
        acc = acc_ref[:, cut] * shrink
        half = chips * tok
        acc = acc + jnp.dot(
            weight_scr[:, :half], near_ref[:, :, v_cut].reshape(half, HD), preferred_element_type=F32
        )
        acc = acc + jnp.dot(
            weight_scr[:, half:], far_ref[:, :, v_cut].reshape(half, HD), preferred_element_type=F32
        )
        att_scr[:, cut] = (acc / (total_ref[:, cut] * shrink + total)).astype(BF16)
    full = w_ref.shape[1]
    width = out_ref.shape[2] if not by_token else full // 16
    step = 2 * width
    for c in range(full // step):
        o = jnp.dot(att_scr[...], w_ref[:, c * step : (c + 1) * step], preferred_element_type=F32)
        if by_token:
            o = o.astype(BF16)
            for r in range(n_z):
                out_ref[lax.rem(r + n_z - z, n_z), :, c * step : (c + 1) * step] = o[r * rows : (r + 1) * rows]
        else:
            o = o.T.astype(BF16)
            for half in range(2):
                block = 2 * c + half
                out_ref[lax.rem(block % n_z + n_z - z, n_z), block // n_z] = o[half * width : (half + 1) * width]


def modulate(wide, meansq, mod_ref, cut):
    return (wide * lax.rsqrt(meansq + 1e-06) * (1.0 + mod_ref[1:2, cut]) + mod_ref[0:1, cut]).astype(BF16)


def first_norm_kernel(place_ref, mod_ref, *refs):
    blocks, (x_ref, normed_ref, turned) = refs[:-3], refs[-3:]
    n_z = len(blocks)
    n_yh, width, tok = blocks[0].shape
    full = x_ref.shape[1]
    for k, block in enumerate(blocks):
        here = lax.rem(place_ref[0] + k, n_z)
        for y in range(n_yh):
            row = pl.multiple_of((y * n_z + here) * width, 64)
            turned[pl.ds(row, width), :] = block[y]
    squares = jnp.zeros((tok, HD), F32)
    for c in range(full // HD):
        cut = slice(c * HD, (c + 1) * HD)
        wide = turned[cut, :].astype(F32).T
        x_ref[:, cut] = wide.astype(BF16)
        squares = squares + wide * wide
    meansq = jnp.sum(squares, axis=1, keepdims=True) * (1.0 / full)
    for c in range(full // HD):
        cut = slice(c * HD, (c + 1) * HD)
        normed_ref[:, cut] = modulate(x_ref[:, cut].astype(F32), meansq, mod_ref, cut)


def second_norm_kernel(place_ref, step_ref, mod_ref, x_ref, *refs):
    blocks, (normed_ref, own_ref) = refs[:-2], refs[-2:]
    n_z = len(blocks)
    rows, full = blocks[0].shape
    width = own_ref.shape[1]
    here = place_ref[1] * width
    start = pl.multiple_of(here // HD * HD, HD)
    shift = here - start
    span = -(-width // HD) * HD
    for k, block in enumerate(blocks):
        row = pl.multiple_of(lax.rem(place_ref[0] + k, n_z) * rows, rows)
        squares = jnp.zeros((rows, HD), F32)
        for c in range(full // HD):
            cut = slice(c * HD, (c + 1) * HD)
            x = x_ref[pl.ds(row, rows), cut].astype(F32) + step_ref[0] * block[:, cut].astype(F32)
            x = x.astype(BF16)
            normed_ref[pl.ds(row, rows), cut] = x
            squares = squares + x.astype(F32) * x.astype(F32)
        meansq = jnp.sum(squares, axis=1, keepdims=True) * (1.0 / full)
        for c in range(full // HD):
            cut = slice(c * HD, (c + 1) * HD)
            x = normed_ref[pl.ds(row, rows), cut].astype(F32)
            normed_ref[pl.ds(row, rows), cut] = modulate(x, meansq, mod_ref, cut)
        window = block[:, pl.ds(start, span)].astype(F32)
        window = jnp.where(shift > 0, pltpu.roll(window, span - HD // 2, 1), window)
        own_ref[pl.ds(row, rows), :] = window[:, :width].astype(BF16)


def per_device(
    latent,
    noise_levels,
    mod_table,
    w_query,
    w_key,
    w_value,
    w_out,
    hist_keys,
    hist_values,
    frame_home,
    hist_list,
    list_count,
):
    tok, width = latent.shape
    level_count, _, full = mod_table.shape
    heads = w_query.shape[1] // HD
    hw = heads * HD
    n_ctx = lax.axis_size(CTX)
    n_chip = lax.axis_size(CHIPS)
    n_z = lax.axis_size("z")
    n_yh = lax.axis_size("yh")
    yh = lax.axis_index("yh")
    core = lax.axis_index("core")
    chip = lax.axis_index(CHIPS)
    z = lax.axis_index("z")
    rows = tok // n_z
    scale = 1.0 / math.sqrt(HD)
    down = [(i, (i - 1) % n_z) for i in range(n_z)]
    up = [(i, (i + 1) % n_z) for i in range(n_z)]

    def ring_gather(block, beside):
        got = {0: block}
        for k in range(1, n_z // 2 + 1):
            got[k] = lax.ppermute(got[k - 1], "z", down)
            if 2 * k < n_z:
                got[-k] = lax.ppermute(got[1 - k], "z", up)
            if k == 1 and beside is not None:
                got[1], got[-1], beside = lax.optimization_barrier((got[1], got[-1], beside))
        return [got[k] if 2 * k <= n_z else got[k - n_z] for k in range(n_z)], beside

    def ring_sum(parts):
        low = parts[n_z // 2]
        high = parts[n_z // 2 - 1]
        for k in range(n_z // 2, 0, -1):
            low = lax.ppermute(low, "z", down)
            if 2 * k > 2:
                high = lax.ppermute(high, "z", up)
            low, high = lax.optimization_barrier((low, high))
            if k > 1:
                low = (low.astype(F32) + parts[n_z - k + 1].astype(F32)).astype(BF16)
            if k > 2:
                high = (high.astype(F32) + parts[k - 2].astype(F32)).astype(BF16)
        return parts[0].astype(F32) + low.astype(F32) + high.astype(F32)

    sigma = (noise_levels[:, 0].astype(F32) + 1.0) / level_count
    steps = sigma[1:] - sigma[:-1]

    slot_per_owner, past_len, _ = hist_keys.shape
    wanted = frame_home[hist_list[0]]
    matched = (wanted // slot_per_owner)[:, None] == jnp.arange(n_ctx, dtype=jnp.int32)[None, :]
    request = jnp.sum(jnp.where(matched, (wanted % slot_per_owner)[:, None], 0), axis=0)
    in_list = jnp.arange(n_ctx, dtype=jnp.int32) < list_count[0]
    valid_owner = jnp.any(matched & in_list[:, None], axis=0)
    picked = lax.all_to_all(request[:, None], CTX, split_axis=0, concat_axis=0, tiled=True)[:, 0]
    hist = jnp.concatenate([hist_keys, hist_values], axis=2)
    asked = hist[picked]

    own = latent.T
    other = lax.ppermute(own, "yh", SWAP)
    pair = jnp.stack([jnp.where(yh == 1, other, own), jnp.where(yh == 1, own, other)])
    blocks, asked = ring_gather(pair, asked)
    past = lax.all_to_all(asked, CTX, split_axis=0, concat_axis=0, tiled=True)

    mods = [mod_table[noise_levels[s, 0]] for s in range(2)]
    smem = pl.BlockSpec(memory_space=pltpu.SMEM)
    vmem = pl.BlockSpec(memory_space=pltpu.VMEM)
    limit = pltpu.CompilerParams(vmem_limit_bytes=24 * 2**20)
    place = jnp.stack([z, lax.axis_index(TP)]).astype(jnp.int32)
    wide = jax.ShapeDtypeStruct((tok, full), BF16)
    x0_full, normed = pl.pallas_call(
        first_norm_kernel,
        out_shape=[wide, wide],
        in_specs=[smem] + [vmem] * (1 + n_z),
        out_specs=[vmem, vmem],
        scratch_shapes=[pltpu.VMEM((full, tok), BF16)],
        compiler_params=limit,
    )(place, mods[0], *blocks)

    chips = jnp.arange(n_chip, dtype=jnp.int32)
    seen_own = chips <= chip
    seen_other = (chips < chip) | ((chips == chip) & (core == 1))
    group_live = jnp.concatenate([seen_own, seen_other]).astype(jnp.int32)
    past_live = valid_owner.astype(jnp.int32)

    def attend(normed, past, by_token):
        k = jnp.dot(normed, w_key, preferred_element_type=F32).astype(BF16)
        v = jnp.dot(normed, w_value, preferred_element_type=F32).astype(BF16)
        kv = jnp.concatenate([k, v], axis=1)
        kv, past = lax.optimization_barrier((kv, past))
        near = lax.all_to_all(
            jnp.broadcast_to(kv[None], (n_chip, tok, 2 * hw)), CHIPS, split_axis=0, concat_axis=0, tiled=True
        )
        q = jnp.dot(normed, w_query, preferred_element_type=F32).astype(BF16)
        stat = jax.ShapeDtypeStruct((tok, hw), F32)
        top, total, acc = pl.pallas_call(
            functools.partial(past_kernel, heads, scale),
            out_shape=[stat, stat, stat],
            in_specs=[smem, vmem, vmem],
            out_specs=[vmem, vmem, vmem],
            scratch_shapes=[
                pltpu.VMEM((tok, n_ctx * past_len), F32),
                pltpu.VMEM((tok, n_ctx * past_len), BF16),
            ],
            compiler_params=limit,
            cost_estimate=pl.CostEstimate(
                flops=4 * tok * n_ctx * past_len * hw,
                bytes_accessed=n_ctx * past_len * hw * 4,
                transcendentals=tok * n_ctx * past_len * heads,
            ),
        )(past_live, q, past)
        near, top, total, acc = lax.optimization_barrier((near, top, total, acc))
        far = lax.ppermute(near, "core", SWAP)
        shape = (n_z, rows, full) if by_token else (n_z, n_yh, width, tok)
        return pl.pallas_call(
            functools.partial(group_kernel, heads, scale, by_token),
            out_shape=jax.ShapeDtypeStruct(shape, BF16),
            in_specs=[smem, smem] + [vmem] * 7,
            out_specs=vmem,
            scratch_shapes=[
                pltpu.VMEM((tok, 2 * n_chip * tok), F32),
                pltpu.VMEM((tok, 2 * n_chip * tok), BF16),
                pltpu.VMEM((tok, hw), BF16),
            ],
            compiler_params=limit,
            cost_estimate=pl.CostEstimate(
                flops=4 * tok * 2 * n_chip * tok * hw + 2 * tok * hw * full,
                bytes_accessed=2 * n_chip * tok * hw * 4 + hw * full * 2 + tok * full * 2,
                transcendentals=tok * 2 * n_chip * tok * heads,
            ),
        )(group_live, place, q, near, far, top, total, acc, w_out)

    part = attend(normed, past, True)
    half = ring_sum([part[k] for k in range(n_z)]).astype(BF16)
    rest = lax.ppermute(half, "yh", SWAP)
    v0_rows = (half.astype(F32) + rest.astype(F32)).astype(BF16)
    blocks, _ = ring_gather(v0_rows, None)
    normed, v0 = pl.pallas_call(
        second_norm_kernel,
        out_shape=[wide, jax.ShapeDtypeStruct((tok, width), BF16)],
        in_specs=[smem, smem] + [vmem] * (2 + n_z),
        out_specs=[vmem, vmem],
        compiler_params=limit,
    )(place, steps[:1], mods[1], x0_full, *blocks)
    x1 = (latent.astype(F32) + steps[0] * v0.astype(F32)).astype(BF16)

    part = attend(normed, past, False)
    halves = ring_sum([part[k] for k in range(n_z)]).astype(BF16)
    keep = jnp.where(yh == 1, halves[1], halves[0])
    give = jnp.where(yh == 1, halves[0], halves[1])
    rest = lax.ppermute(give, "yh", SWAP)
    v1 = (keep.astype(F32) + rest.astype(F32)).astype(BF16).T
    x2 = (x1.astype(F32) + steps[1] * v1.astype(F32)).astype(BF16)
    return x2, jnp.stack([v0, v1])


def solution(mesh):
    fine = Mesh(mesh.devices.reshape(2, 4, 2, 2, 8), ("yl", "x", "core", "yh", "z"))
    return jax.shard_map(
        per_device,
        mesh=fine,
        in_specs=(
            P(CTX, TP),
            P(None, CTX),
            P(),
            P(None, TP),
            P(None, TP),
            P(None, TP),
            P(TP, None),
            P(CTX, None, TP),
            P(CTX, None, TP),
            P(),
            P(CTX, None),
            P(CTX),
        ),
        out_specs=(P(CTX, TP), P(None, CTX, TP)),
        check_vma=False,
    )
```

```python
import functools
import math

import jax
import jax.numpy as jnp
from jax import lax
from jax.experimental import pallas as pl
from jax.experimental.pallas import tpu as pltpu
from jax.sharding import Mesh, PartitionSpec as P

HD = 128
CTX = ("yl", "x", "core")
CHIPS = ("yl", "x")
TP = ("yh", "z")
F32, BF16 = jnp.float32, jnp.bfloat16
LOW = -1e30
SWAP = [(0, 1), (1, 0)]


def block_scores(q, live_ref, base, keys, score_scr, scale):
    top = None
    for j, key in enumerate(keys):
        s = lax.dot_general(q, key, (((1,), (1,)), ((), ())), preferred_element_type=F32) * scale
        s = s + jnp.where(live_ref[base + j] > 0, 0.0, LOW)
        score_scr[:, j * HD : (j + 1) * HD] = s
        top = s if top is None else jnp.maximum(top, s)
    return jnp.max(top, axis=1, keepdims=True)


def weigh(score_scr, weight_scr, top, blocks):
    total = None
    for j in range(blocks):
        w = jnp.exp(score_scr[:, j * HD : (j + 1) * HD] - top)
        weight_scr[:, j * HD : (j + 1) * HD] = w.astype(BF16)
        total = w if total is None else total + w
    return jnp.sum(total, axis=1, keepdims=True)


def past_kernel(heads, scale, live_ref, q_ref, past_ref, top_ref, total_ref, acc_ref, score_scr, weight_scr):
    blocks, past_len, _ = past_ref.shape
    for h in range(heads):
        cut = slice(h * HD, (h + 1) * HD)
        v_cut = slice((heads + h) * HD, (heads + h + 1) * HD)
        keys = [past_ref[j, :, cut] for j in range(blocks)]
        top = block_scores(q_ref[:, cut], live_ref, 0, keys, score_scr, scale)
        total = weigh(score_scr, weight_scr, top, blocks)
        values = past_ref[:, :, v_cut].reshape(blocks * past_len, HD)
        acc_ref[:, cut] = jnp.dot(weight_scr[...], values, preferred_element_type=F32)
        top_ref[:, cut] = jnp.broadcast_to(top, (q_ref.shape[0], HD))
        total_ref[:, cut] = jnp.broadcast_to(total, (q_ref.shape[0], HD))


def group_kernel(
    heads, scale, by_token, live_ref, place_ref, q_ref, near_ref, far_ref, top_ref, total_ref, acc_ref, w_ref,
    out_ref, score_scr, weight_scr, att_scr,
):
    chips, tok, _ = near_ref.shape
    z = place_ref[0]
    n_z = out_ref.shape[0]
    rows = tok // n_z
    for h in range(heads):
        cut = slice(h * HD, (h + 1) * HD)
        v_cut = slice((heads + h) * HD, (heads + h + 1) * HD)
        keys = [near_ref[j, :, cut] for j in range(chips)] + [far_ref[j, :, cut] for j in range(chips)]
        top = block_scores(q_ref[:, cut], live_ref, 0, keys, score_scr, scale)
        past_top = top_ref[:, cut]
        new_top = jnp.maximum(past_top, top)
        total = weigh(score_scr, weight_scr, new_top, 2 * chips)
        shrink = jnp.exp(past_top - new_top)
        acc = acc_ref[:, cut] * shrink
        half = chips * tok
        acc = acc + jnp.dot(
            weight_scr[:, :half], near_ref[:, :, v_cut].reshape(half, HD), preferred_element_type=F32
        )
        acc = acc + jnp.dot(
            weight_scr[:, half:], far_ref[:, :, v_cut].reshape(half, HD), preferred_element_type=F32
        )
        att_scr[:, cut] = (acc / (total_ref[:, cut] * shrink + total)).astype(BF16)
    full = w_ref.shape[1]
    width = out_ref.shape[2] if not by_token else full // 16
    step = 2 * width
    for c in range(full // step):
        o = jnp.dot(att_scr[...], w_ref[:, c * step : (c + 1) * step], preferred_element_type=F32)
        if by_token:
            o = o.astype(BF16)
            for r in range(n_z):
                out_ref[lax.rem(r + n_z - z, n_z), :, c * step : (c + 1) * step] = o[r * rows : (r + 1) * rows]
        else:
            o = o.T.astype(BF16)
            for half in range(2):
                block = 2 * c + half
                y = lax.rem(block // n_z + place_ref[2], 2)
                out_ref[lax.rem(block % n_z + n_z - z, n_z), y] = o[half * width : (half + 1) * width]


def pick_kernel(picked_ref, keys_ref, values_ref, out_ref):
    hw = keys_ref.shape[2]
    for d in range(out_ref.shape[0]):
        out_ref[d, :, :hw] = keys_ref[picked_ref[d]]
        out_ref[d, :, hw:] = values_ref[picked_ref[d]]


def modulate(wide, meansq, mod_ref, cut):
    return (wide * lax.rsqrt(meansq + 1e-06) * (1.0 + mod_ref[1:2, cut]) + mod_ref[0:1, cut]).astype(BF16)


def first_norm_kernel(place_ref, mod_ref, *refs):
    blocks, (x_ref, normed_ref, turned) = refs[:-3], refs[-3:]
    n_z = len(blocks)
    n_yh, width, tok = blocks[0].shape
    full = x_ref.shape[1]
    for k, block in enumerate(blocks):
        here = lax.rem(place_ref[0] + k, n_z)
        for y in range(n_yh):
            row = pl.multiple_of((lax.rem(place_ref[2] + y, n_yh) * n_z + here) * width, 64)
            turned[pl.ds(row, width), :] = block[y]
    squares = jnp.zeros((tok, HD), F32)
    for c in range(full // HD):
        cut = slice(c * HD, (c + 1) * HD)
        wide = turned[cut, :].astype(F32).T
        x_ref[:, cut] = wide.astype(BF16)
        squares = squares + wide * wide
    meansq = jnp.sum(squares, axis=1, keepdims=True) * (1.0 / full)
    for c in range(full // HD):
        cut = slice(c * HD, (c + 1) * HD)
        normed_ref[:, cut] = modulate(x_ref[:, cut].astype(F32), meansq, mod_ref, cut)


def second_norm_kernel(place_ref, step_ref, mod_ref, x_ref, *refs):
    blocks, (normed_ref, own_ref) = refs[:-2], refs[-2:]
    n_z = len(blocks)
    rows, full = blocks[0].shape
    width = own_ref.shape[1]
    here = place_ref[1] * width
    start = pl.multiple_of(here // HD * HD, HD)
    shift = here - start
    span = -(-width // HD) * HD
    for k, block in enumerate(blocks):
        row = pl.multiple_of(lax.rem(place_ref[0] + k, n_z) * rows, rows)
        squares = jnp.zeros((rows, HD), F32)
        for c in range(full // HD):
            cut = slice(c * HD, (c + 1) * HD)
            x = x_ref[pl.ds(row, rows), cut].astype(F32) + step_ref[0] * block[:, cut].astype(F32)
            x = x.astype(BF16)
            normed_ref[pl.ds(row, rows), cut] = x
            squares = squares + x.astype(F32) * x.astype(F32)
        meansq = jnp.sum(squares, axis=1, keepdims=True) * (1.0 / full)
        for c in range(full // HD):
            cut = slice(c * HD, (c + 1) * HD)
            x = normed_ref[pl.ds(row, rows), cut].astype(F32)
            normed_ref[pl.ds(row, rows), cut] = modulate(x, meansq, mod_ref, cut)
        window = block[:, pl.ds(start, span)].astype(F32)
        window = jnp.where(shift > 0, pltpu.roll(window, span - HD // 2, 1), window)
        own_ref[pl.ds(row, rows), :] = window[:, :width].astype(BF16)


def per_device(
    latent,
    noise_levels,
    mod_table,
    w_query,
    w_key,
    w_value,
    w_out,
    hist_keys,
    hist_values,
    frame_home,
    hist_list,
    list_count,
):
    tok, width = latent.shape
    level_count, _, full = mod_table.shape
    heads = w_query.shape[1] // HD
    hw = heads * HD
    n_ctx = lax.axis_size(CTX)
    n_chip = lax.axis_size(CHIPS)
    n_z = lax.axis_size("z")
    n_yh = lax.axis_size("yh")
    yh = lax.axis_index("yh")
    core = lax.axis_index("core")
    chip = lax.axis_index(CHIPS)
    z = lax.axis_index("z")
    rows = tok // n_z
    scale = 1.0 / math.sqrt(HD)
    down = [(i, (i - 1) % n_z) for i in range(n_z)]
    up = [(i, (i + 1) % n_z) for i in range(n_z)]

    cross = [(i, (i + n_z) % (n_yh * n_z)) for i in range(n_yh * n_z)]
    cross_down = [(y * n_z + a, (1 - y) * n_z + b) for y in range(n_yh) for a, b in down]
    cross_up = [(y * n_z + a, (1 - y) * n_z + b) for y in range(n_yh) for a, b in up]

    def ring_gather(got):
        for k in range(1, n_z // 2 + 1):
            if k not in got:
                got[k] = lax.ppermute(got[k - 1], "z", down)
            if 2 * k < n_z and -k not in got:
                got[-k] = lax.ppermute(got[1 - k], "z", up)
        return [got[k] if 2 * k <= n_z else got[k - n_z] for k in range(n_z)]

    def add(a, b):
        return (a.astype(F32) + b.astype(F32)).astype(BF16)

    def ring_sum(parts):
        low, high = parts[n_z // 2], parts[n_z // 2 - 1]
        for k in range(n_z // 2 - 1, 0, -1):
            low_in = lax.ppermute(low, "z", down)
            if k > 1:
                high_in = lax.ppermute(high, "z", up)
                low_in, high = lax.optimization_barrier((low_in, high_in))
                high = add(high, parts[k - 1])
            low = add(low_in, parts[n_z - k])
        return low, high

    sigma = (noise_levels[:, 0].astype(F32) + 1.0) / level_count
    steps = sigma[1:] - sigma[:-1]

    slot_per_owner, past_len, _ = hist_keys.shape
    frames = jnp.arange(frame_home.shape[0], dtype=jnp.int32)
    wanted = jnp.sum(jnp.where(hist_list[0][:, None] == frames[None, :], frame_home[None, :], 0), axis=1)
    matched = (wanted // slot_per_owner)[:, None] == jnp.arange(n_ctx, dtype=jnp.int32)[None, :]
    request = jnp.sum(jnp.where(matched, (wanted % slot_per_owner)[:, None], 0), axis=0)
    in_list = jnp.arange(n_ctx, dtype=jnp.int32) < list_count[0]
    valid_owner = jnp.any(matched & in_list[:, None], axis=0)
    picked = lax.all_to_all(request[:, None], CTX, split_axis=0, concat_axis=0, tiled=True)[:, 0]
    smem = pl.BlockSpec(memory_space=pltpu.SMEM)
    vmem = pl.BlockSpec(memory_space=pltpu.VMEM)
    limit = pltpu.CompilerParams(vmem_limit_bytes=12 * 2**20)
    asked = pl.pallas_call(
        pick_kernel,
        out_shape=jax.ShapeDtypeStruct((n_ctx, past_len, 2 * hw), BF16),
        in_specs=[smem, vmem, vmem],
        out_specs=vmem,
        compiler_params=limit,
    )(picked, hist_keys, hist_values)
    past = lax.all_to_all(asked, CTX, split_axis=0, concat_axis=0, tiled=True)

    own = latent.T
    first = {
        0: (own, lax.ppermute(own, TP, cross)),
        1: (lax.ppermute(own, "z", down), lax.ppermute(own, TP, cross_down)),
        -1: (lax.ppermute(own, "z", up), lax.ppermute(own, TP, cross_up)),
    }
    blocks = ring_gather({k: jnp.stack(pair) for k, pair in first.items()})

    mods = [mod_table[noise_levels[s, 0]] for s in range(2)]
    place = jnp.stack([z, lax.axis_index(TP), yh]).astype(jnp.int32)
    wide = jax.ShapeDtypeStruct((tok, full), BF16)
    x0_full, normed = pl.pallas_call(
        first_norm_kernel,
        out_shape=[wide, wide],
        in_specs=[smem] + [vmem] * (1 + n_z),
        out_specs=[vmem, vmem],
        scratch_shapes=[pltpu.VMEM((full, tok), BF16)],
        compiler_params=limit,
    )(place, mods[0], *blocks)

    chips = jnp.arange(n_chip, dtype=jnp.int32)
    seen_own = chips <= chip
    seen_other = (chips < chip) | ((chips == chip) & (core == 1))
    group_live = jnp.concatenate([seen_own, seen_other]).astype(jnp.int32)
    past_live = valid_owner.astype(jnp.int32)

    def attend(normed, past, by_token):
        k = jnp.dot(normed, w_key, preferred_element_type=F32).astype(BF16)
        v = jnp.dot(normed, w_value, preferred_element_type=F32).astype(BF16)
        kv = jnp.concatenate([k, v], axis=1)
        kv, past = lax.optimization_barrier((kv, past))
        near = lax.all_to_all(
            jnp.broadcast_to(kv[None], (n_chip, tok, 2 * hw)), CHIPS, split_axis=0, concat_axis=0, tiled=True
        )
        q = jnp.dot(normed, w_query, preferred_element_type=F32).astype(BF16)
        stat = jax.ShapeDtypeStruct((tok, hw), F32)
        top, total, acc = pl.pallas_call(
            functools.partial(past_kernel, heads, scale),
            out_shape=[stat, stat, stat],
            in_specs=[smem, vmem, vmem],
            out_specs=[vmem, vmem, vmem],
            scratch_shapes=[
                pltpu.VMEM((tok, n_ctx * past_len), F32),
                pltpu.VMEM((tok, n_ctx * past_len), BF16),
            ],
            compiler_params=limit,
            cost_estimate=pl.CostEstimate(
                flops=4 * tok * n_ctx * past_len * hw,
                bytes_accessed=n_ctx * past_len * hw * 4,
                transcendentals=tok * n_ctx * past_len * heads,
            ),
        )(past_live, q, past)
        near, top, total, acc = lax.optimization_barrier((near, top, total, acc))
        far = lax.ppermute(near, "core", SWAP)
        shape = (n_z, rows, full) if by_token else (n_z, n_yh, width, tok)
        return pl.pallas_call(
            functools.partial(group_kernel, heads, scale, by_token),
            out_shape=jax.ShapeDtypeStruct(shape, BF16),
            in_specs=[smem, smem] + [vmem] * 7,
            out_specs=vmem,
            scratch_shapes=[
                pltpu.VMEM((tok, 2 * n_chip * tok), F32),
                pltpu.VMEM((tok, 2 * n_chip * tok), BF16),
                pltpu.VMEM((tok, hw), BF16),
            ],
            compiler_params=limit,
            cost_estimate=pl.CostEstimate(
                flops=4 * tok * 2 * n_chip * tok * hw + 2 * tok * hw * full,
                bytes_accessed=2 * n_chip * tok * hw * 4 + hw * full * 2 + tok * full * 2,
                transcendentals=tok * 2 * n_chip * tok * heads,
            ),
        )(group_live, place, q, near, far, top, total, acc, w_out)

    part = attend(normed, past, True)
    away = lax.ppermute(part[0], TP, cross)
    low, high = ring_sum([part[k] for k in range(n_z)])
    here = [part[0], lax.ppermute(low, "z", down), lax.ppermute(high, "z", up)]
    there = [away, lax.ppermute(low, TP, cross_down), lax.ppermute(high, TP, cross_up)]
    here, there = [sum(x.astype(F32) for x in side) for side in (here, there)]
    v0_rows = (here + there).astype(BF16)
    blocks = ring_gather({0: v0_rows})
    normed, v0 = pl.pallas_call(
        second_norm_kernel,
        out_shape=[wide, jax.ShapeDtypeStruct((tok, width), BF16)],
        in_specs=[smem, smem] + [vmem] * (2 + n_z),
        out_specs=[vmem, vmem],
        compiler_params=limit,
    )(place, steps[:1], mods[1], x0_full, *blocks)
    x1 = (latent.astype(F32) + steps[0] * v0.astype(F32)).astype(BF16)

    part = attend(normed, past, False)
    away = lax.ppermute(part[0, 1], TP, cross)
    low, high = ring_sum([part[k] for k in range(n_z)])
    here = [part[0, 0], lax.ppermute(low[0], "z", down), lax.ppermute(high[0], "z", up)]
    there = [away, lax.ppermute(low[1], TP, cross_down), lax.ppermute(high[1], TP, cross_up)]
    v1 = sum(x.astype(F32) for x in here + there).astype(BF16).T
    x2 = (x1.astype(F32) + steps[1] * v1.astype(F32)).astype(BF16)
    return x2, jnp.stack([v0, v1])


def solution(mesh):
    fine = Mesh(mesh.devices.reshape(2, 4, 2, 2, 8), ("yl", "x", "core", "yh", "z"))
    return jax.shard_map(
        per_device,
        mesh=fine,
        in_specs=(
            P(CTX, TP),
            P(None, CTX),
            P(),
            P(None, TP),
            P(None, TP),
            P(None, TP),
            P(TP, None),
            P(CTX, None, TP),
            P(CTX, None, TP),
            P(),
            P(CTX, None),
            P(CTX),
        ),
        out_specs=(P(CTX, TP), P(None, CTX, TP)),
        check_vma=False,
    )
```

```python
import functools
import math

import jax
import jax.numpy as jnp
from jax import lax
from jax.experimental import pallas as pl
from jax.experimental.pallas import tpu as pltpu
from jax.sharding import Mesh, PartitionSpec as P

HD = 128
CTX = ("yl", "x", "core")
CHIPS = ("yl", "x")
TP = ("yh", "z")
F32, BF16 = jnp.float32, jnp.bfloat16
LOW = -1e30
SWAP = [(0, 1), (1, 0)]


def block_scores(q, live_ref, base, keys, score_scr, scale):
    top = None
    for j, key in enumerate(keys):
        s = lax.dot_general(q, key, (((1,), (1,)), ((), ())), preferred_element_type=F32) * scale
        s = s + jnp.where(live_ref[base + j] > 0, 0.0, LOW)
        score_scr[:, j * HD : (j + 1) * HD] = s
        top = s if top is None else jnp.maximum(top, s)
    return jnp.max(top, axis=1, keepdims=True)


def weigh(score_scr, weight_scr, top, blocks):
    total = None
    for j in range(blocks):
        w = jnp.exp(score_scr[:, j * HD : (j + 1) * HD] - top)
        weight_scr[:, j * HD : (j + 1) * HD] = w.astype(BF16)
        total = w if total is None else total + w
    return jnp.sum(total, axis=1, keepdims=True)


def past_kernel(heads, scale, live_ref, q_ref, past_ref, top_ref, total_ref, acc_ref, score_scr, weight_scr):
    blocks, _, past_len, _ = past_ref.shape
    for h in range(heads):
        cut = slice(h * HD, (h + 1) * HD)
        keys = [past_ref[j, 0, :, cut] for j in range(blocks)]
        top = block_scores(q_ref[:, cut], live_ref, 0, keys, score_scr, scale)
        total = weigh(score_scr, weight_scr, top, blocks)
        values = past_ref[:, 1, :, cut].reshape(blocks * past_len, HD)
        acc_ref[:, cut] = jnp.dot(weight_scr[...], values, preferred_element_type=F32)
        top_ref[:, cut] = jnp.broadcast_to(top, (q_ref.shape[0], HD))
        total_ref[:, cut] = jnp.broadcast_to(total, (q_ref.shape[0], HD))


def group_kernel(
    heads, scale, by_token, live_ref, place_ref, q_ref, near_ref, far_ref, top_ref, total_ref, acc_ref, w_out_ref,
    out_ref, score_scr, weight_scr, att_scr, w_ref, sem,
):
    fetch = pltpu.make_async_copy(w_out_ref, w_ref, sem)
    fetch.start()
    chips, tok, _ = near_ref.shape
    z = place_ref[0]
    n_z = out_ref.shape[0]
    rows = tok // n_z
    for h in range(heads):
        cut = slice(h * HD, (h + 1) * HD)
        v_cut = slice((heads + h) * HD, (heads + h + 1) * HD)
        keys = [near_ref[j, :, cut] for j in range(chips)] + [far_ref[j, :, cut] for j in range(chips)]
        top = block_scores(q_ref[:, cut], live_ref, 0, keys, score_scr, scale)
        past_top = top_ref[:, cut]
        new_top = jnp.maximum(past_top, top)
        total = weigh(score_scr, weight_scr, new_top, 2 * chips)
        shrink = jnp.exp(past_top - new_top)
        acc = acc_ref[:, cut] * shrink
        half = chips * tok
        acc = acc + jnp.dot(
            weight_scr[:, :half], near_ref[:, :, v_cut].reshape(half, HD), preferred_element_type=F32
        )
        acc = acc + jnp.dot(
            weight_scr[:, half:], far_ref[:, :, v_cut].reshape(half, HD), preferred_element_type=F32
        )
        att_scr[:, cut] = (acc / (total_ref[:, cut] * shrink + total)).astype(BF16)
    fetch.wait()
    full = w_ref.shape[1]
    width = out_ref.shape[2] if not by_token else full // 16
    step = 2 * width
    for c in range(full // step):
        o = jnp.dot(att_scr[...], w_ref[:, c * step : (c + 1) * step], preferred_element_type=F32)
        if by_token:
            o = o.astype(BF16)
            for r in range(n_z):
                out_ref[lax.rem(r + n_z - z, n_z), :, c * step : (c + 1) * step] = o[r * rows : (r + 1) * rows]
        else:
            o = o.T.astype(BF16)
            for half in range(2):
                block = 2 * c + half
                y = lax.rem(block // n_z + place_ref[2], 2)
                out_ref[lax.rem(block % n_z + n_z - z, n_z), y] = o[half * width : (half + 1) * width]


def pick_kernel(picked_ref, keys_ref, values_ref, out_ref, sems):
    copies = []
    for d in range(out_ref.shape[0]):
        for i, ref in enumerate((keys_ref, values_ref)):
            copies.append(pltpu.make_async_copy(ref.at[picked_ref[d]], out_ref.at[d, i], sems.at[d, i]))
    for copy in copies:
        copy.start()
    for copy in copies:
        copy.wait()


def modulate(wide, meansq, mod_ref, cut):
    return (wide * lax.rsqrt(meansq + 1e-06) * (1.0 + mod_ref[1:2, cut]) + mod_ref[0:1, cut]).astype(BF16)


def project(normed_ref, weights, fetches, kv_ref):
    for i, (weight, fetch) in enumerate(zip(weights, fetches)):
        fetch.wait()
        width = weight.shape[1]
        out = jnp.dot(normed_ref[...], weight[...], preferred_element_type=F32).astype(BF16)
        for c in range(kv_ref.shape[0]):
            kv_ref[c, :, i * width : (i + 1) * width] = out


def first_norm_kernel(place_ref, mod_ref, w_key_ref, w_value_ref, *refs):
    blocks, (x_ref, normed_ref, kv_ref, turned, k_scr, v_scr, sems) = refs[:-7], refs[-7:]
    fetches = [
        pltpu.make_async_copy(w_key_ref, k_scr, sems.at[0]),
        pltpu.make_async_copy(w_value_ref, v_scr, sems.at[1]),
    ]
    for fetch in fetches:
        fetch.start()
    n_z = len(blocks)
    n_yh, width, tok = blocks[0].shape
    full = x_ref.shape[1]
    for k, block in enumerate(blocks):
        here = lax.rem(place_ref[0] + k, n_z)
        for y in range(n_yh):
            row = pl.multiple_of((lax.rem(place_ref[2] + y, n_yh) * n_z + here) * width, 64)
            turned[pl.ds(row, width), :] = block[y]
    squares = jnp.zeros((tok, HD), F32)
    for c in range(full // HD):
        cut = slice(c * HD, (c + 1) * HD)
        wide = turned[cut, :].astype(F32).T
        x_ref[:, cut] = wide.astype(BF16)
        squares = squares + wide * wide
    meansq = jnp.sum(squares, axis=1, keepdims=True) * (1.0 / full)
    for c in range(full // HD):
        cut = slice(c * HD, (c + 1) * HD)
        normed_ref[:, cut] = modulate(x_ref[:, cut].astype(F32), meansq, mod_ref, cut)
    project(normed_ref, (k_scr, v_scr), fetches, kv_ref)


def second_norm_kernel(place_ref, step_ref, mod_ref, w_key_ref, w_value_ref, x_ref, *refs):
    blocks, (normed_ref, own_ref, kv_ref, k_scr, v_scr, sems) = refs[:-6], refs[-6:]
    fetches = [
        pltpu.make_async_copy(w_key_ref, k_scr, sems.at[0]),
        pltpu.make_async_copy(w_value_ref, v_scr, sems.at[1]),
    ]
    for fetch in fetches:
        fetch.start()
    n_z = len(blocks)
    rows, full = blocks[0].shape
    width = own_ref.shape[1]
    here = place_ref[1] * width
    start = pl.multiple_of(here // HD * HD, HD)
    shift = here - start
    span = -(-width // HD) * HD
    for k, block in enumerate(blocks):
        row = pl.multiple_of(lax.rem(place_ref[0] + k, n_z) * rows, rows)
        squares = jnp.zeros((rows, HD), F32)
        for c in range(full // HD):
            cut = slice(c * HD, (c + 1) * HD)
            x = x_ref[pl.ds(row, rows), cut].astype(F32) + step_ref[0] * block[:, cut].astype(F32)
            x = x.astype(BF16)
            normed_ref[pl.ds(row, rows), cut] = x
            squares = squares + x.astype(F32) * x.astype(F32)
        meansq = jnp.sum(squares, axis=1, keepdims=True) * (1.0 / full)
        for c in range(full // HD):
            cut = slice(c * HD, (c + 1) * HD)
            x = normed_ref[pl.ds(row, rows), cut].astype(F32)
            normed_ref[pl.ds(row, rows), cut] = modulate(x, meansq, mod_ref, cut)
        window = block[:, pl.ds(start, span)].astype(F32)
        window = jnp.where(shift > 0, pltpu.roll(window, span - HD // 2, 1), window)
        own_ref[pl.ds(row, rows), :] = window[:, :width].astype(BF16)
    project(normed_ref, (k_scr, v_scr), fetches, kv_ref)


def per_device(
    latent,
    noise_levels,
    mod_table,
    w_query,
    w_key,
    w_value,
    w_out,
    hist_keys,
    hist_values,
    frame_home,
    hist_list,
    list_count,
):
    tok, width = latent.shape
    level_count, _, full = mod_table.shape
    heads = w_query.shape[1] // HD
    hw = heads * HD
    n_ctx = lax.axis_size(CTX)
    n_chip = lax.axis_size(CHIPS)
    n_z = lax.axis_size("z")
    n_yh = lax.axis_size("yh")
    yh = lax.axis_index("yh")
    core = lax.axis_index("core")
    chip = lax.axis_index(CHIPS)
    z = lax.axis_index("z")
    rows = tok // n_z
    scale = 1.0 / math.sqrt(HD)
    down = [(i, (i - 1) % n_z) for i in range(n_z)]
    up = [(i, (i + 1) % n_z) for i in range(n_z)]

    def ring_gather(block, beside):
        got = {0: block}
        for k in range(1, n_z // 2 + 1):
            got[k] = lax.ppermute(got[k - 1], "z", down)
            if 2 * k < n_z:
                got[-k] = lax.ppermute(got[1 - k], "z", up)
            if k == 1 and beside is not None:
                got[1], got[-1], beside = lax.optimization_barrier((got[1], got[-1], beside))
        return [got[k] if 2 * k <= n_z else got[k - n_z] for k in range(n_z)], beside

    def add(a, b):
        return (a.astype(F32) + b.astype(F32)).astype(BF16)

    def ring_sum(parts):
        low, high, before = parts[n_z // 2], parts[n_z // 2 - 1], None
        for k in range(n_z // 2, 0, -1):
            low = lax.ppermute(low, "z", down)
            if k > 1:
                low = add(low, parts[n_z - k + 1])
            if before is not None:
                low, _ = lax.optimization_barrier((low, before))
            if k > 1:
                before = high = lax.ppermute(high, "z", up)
            if k > 2:
                high = add(high, parts[k - 2])
        return parts[0].astype(F32) + low.astype(F32) + high.astype(F32)

    sigma = (noise_levels[:, 0].astype(F32) + 1.0) / level_count
    steps = sigma[1:] - sigma[:-1]

    slot_per_owner, past_len, _ = hist_keys.shape
    frames = jnp.arange(frame_home.shape[0], dtype=jnp.int32)
    wanted = jnp.sum(jnp.where(hist_list[0][:, None] == frames[None, :], frame_home[None, :], 0), axis=1)
    matched = (wanted // slot_per_owner)[:, None] == jnp.arange(n_ctx, dtype=jnp.int32)[None, :]
    request = jnp.sum(jnp.where(matched, (wanted % slot_per_owner)[:, None], 0), axis=0)
    in_list = jnp.arange(n_ctx, dtype=jnp.int32) < list_count[0]
    valid_owner = jnp.any(matched & in_list[:, None], axis=0)
    picked = lax.all_to_all(request[:, None], CTX, split_axis=0, concat_axis=0, tiled=True)[:, 0]
    smem = pl.BlockSpec(memory_space=pltpu.SMEM)
    vmem = pl.BlockSpec(memory_space=pltpu.VMEM)
    hbm = pl.BlockSpec(memory_space=pl.ANY)
    limit = pltpu.CompilerParams(vmem_limit_bytes=20 * 2**20)

    own = latent.T
    pair = jnp.stack([own, lax.ppermute(own, "yh", SWAP)])
    blocks, picked = ring_gather(pair, picked)
    asked = pl.pallas_call(
        pick_kernel,
        out_shape=jax.ShapeDtypeStruct((n_ctx, 2, past_len, hw), BF16),
        in_specs=[smem, hbm, hbm],
        out_specs=vmem,
        scratch_shapes=[pltpu.SemaphoreType.DMA((n_ctx, 2))],
        compiler_params=limit,
    )(picked, hist_keys, hist_values)
    past = lax.all_to_all(asked, CTX, split_axis=0, concat_axis=0, tiled=True)

    mods = [mod_table[noise_levels[s, 0]] for s in range(2)]
    place = jnp.stack([z, lax.axis_index(TP), yh]).astype(jnp.int32)
    wide = jax.ShapeDtypeStruct((tok, full), BF16)
    kv_copies = jax.ShapeDtypeStruct((n_chip, tok, 2 * hw), BF16)
    kv_scratch = [pltpu.VMEM((full, hw), BF16), pltpu.VMEM((full, hw), BF16), pltpu.SemaphoreType.DMA((2,))]
    x0_full, normed, kv = pl.pallas_call(
        first_norm_kernel,
        out_shape=[wide, wide, kv_copies],
        in_specs=[smem, vmem, hbm, hbm] + [vmem] * n_z,
        out_specs=[vmem] * 3,
        scratch_shapes=[pltpu.VMEM((full, tok), BF16)] + kv_scratch,
        compiler_params=limit,
    )(place, mods[0], w_key, w_value, *blocks)

    chips = jnp.arange(n_chip, dtype=jnp.int32)
    seen_own = chips <= chip
    seen_other = (chips < chip) | ((chips == chip) & (core == 1))
    group_live = jnp.concatenate([seen_own, seen_other]).astype(jnp.int32)
    past_live = valid_owner.astype(jnp.int32)

    def attend(normed, kv, past, by_token):
        kv, past = lax.optimization_barrier((kv, past))
        near = lax.all_to_all(kv, CHIPS, split_axis=0, concat_axis=0, tiled=True)
        q = jnp.dot(normed, w_query, preferred_element_type=F32).astype(BF16)
        stat = jax.ShapeDtypeStruct((tok, hw), F32)
        top, total, acc = pl.pallas_call(
            functools.partial(past_kernel, heads, scale),
            out_shape=[stat, stat, stat],
            in_specs=[smem, vmem, vmem],
            out_specs=[vmem, vmem, vmem],
            scratch_shapes=[
                pltpu.VMEM((tok, n_ctx * past_len), F32),
                pltpu.VMEM((tok, n_ctx * past_len), BF16),
            ],
            compiler_params=limit,
            cost_estimate=pl.CostEstimate(
                flops=4 * tok * n_ctx * past_len * hw,
                bytes_accessed=n_ctx * past_len * hw * 4,
                transcendentals=tok * n_ctx * past_len * heads,
            ),
        )(past_live, q, past)
        near, top, total, acc = lax.optimization_barrier((near, top, total, acc))
        far = lax.ppermute(near, "core", SWAP)
        shape = (n_z, rows, full) if by_token else (n_z, n_yh, width, tok)
        return pl.pallas_call(
            functools.partial(group_kernel, heads, scale, by_token),
            out_shape=jax.ShapeDtypeStruct(shape, BF16),
            in_specs=[smem, smem] + [vmem] * 6 + [hbm],
            out_specs=vmem,
            scratch_shapes=[
                pltpu.VMEM((tok, 2 * n_chip * tok), F32),
                pltpu.VMEM((tok, 2 * n_chip * tok), BF16),
                pltpu.VMEM((tok, hw), BF16),
                pltpu.VMEM((hw, full), BF16),
                pltpu.SemaphoreType.DMA,
            ],
            compiler_params=limit,
            cost_estimate=pl.CostEstimate(
                flops=4 * tok * 2 * n_chip * tok * hw + 2 * tok * hw * full,
                bytes_accessed=2 * n_chip * tok * hw * 4 + hw * full * 2 + tok * full * 2,
                transcendentals=tok * 2 * n_chip * tok * heads,
            ),
        )(group_live, place, q, near, far, top, total, acc, w_out)

    part = attend(normed, kv, past, True)
    half = ring_sum([part[k] for k in range(n_z)]).astype(BF16)
    rest = lax.ppermute(half, "yh", SWAP)
    v0_rows = (half.astype(F32) + rest.astype(F32)).astype(BF16)
    blocks, _ = ring_gather(v0_rows, None)
    normed, v0, kv = pl.pallas_call(
        second_norm_kernel,
        out_shape=[wide, jax.ShapeDtypeStruct((tok, width), BF16), kv_copies],
        in_specs=[smem, smem, vmem, hbm, hbm] + [vmem] * (1 + n_z),
        out_specs=[vmem] * 3,
        scratch_shapes=kv_scratch,
        compiler_params=limit,
    )(place, steps[:1], mods[1], w_key, w_value, x0_full, *blocks)
    x1 = (latent.astype(F32) + steps[0] * v0.astype(F32)).astype(BF16)

    part = attend(normed, kv, past, False)
    halves = ring_sum([part[k] for k in range(n_z)])
    rest = lax.ppermute(halves[1].astype(BF16), "yh", SWAP)
    v1 = (halves[0] + rest.astype(F32)).astype(BF16).T
    x2 = (x1.astype(F32) + steps[1] * v1.astype(F32)).astype(BF16)
    return x2, jnp.stack([v0, v1])


def solution(mesh):
    fine = Mesh(mesh.devices.reshape(2, 4, 2, 2, 8), ("yl", "x", "core", "yh", "z"))
    return jax.shard_map(
        per_device,
        mesh=fine,
        in_specs=(
            P(CTX, TP),
            P(None, CTX),
            P(),
            P(None, TP),
            P(None, TP),
            P(None, TP),
            P(TP, None),
            P(CTX, None, TP),
            P(CTX, None, TP),
            P(),
            P(CTX, None),
            P(CTX),
        ),
        out_specs=(P(CTX, TP), P(None, CTX, TP)),
        check_vma=False,
    )
```

```python
import functools
import math

import jax
import jax.numpy as jnp
from jax import lax
from jax.experimental import pallas as pl
from jax.experimental.pallas import tpu as pltpu
from jax.sharding import Mesh, PartitionSpec as P

HD = 128
CTX = ("yl", "x", "core")
CHIPS = ("yl", "x")
TP = ("yh", "z")
F32, BF16 = jnp.float32, jnp.bfloat16
LOW = -1e30
SWAP = [(0, 1), (1, 0)]


def block_scores(q, live_ref, base, keys, score_scr, scale):
    top = None
    for j, key in enumerate(keys):
        s = lax.dot_general(q, key, (((1,), (1,)), ((), ())), preferred_element_type=F32) * scale
        s = s + jnp.where(live_ref[base + j] > 0, 0.0, LOW)
        score_scr[:, j * HD : (j + 1) * HD] = s
        top = s if top is None else jnp.maximum(top, s)
    return jnp.max(top, axis=1, keepdims=True)


def weigh(score_scr, weight_scr, top, blocks):
    total = None
    for j in range(blocks):
        w = jnp.exp(score_scr[:, j * HD : (j + 1) * HD] - top)
        weight_scr[:, j * HD : (j + 1) * HD] = w.astype(BF16)
        total = w if total is None else total + w
    return jnp.sum(total, axis=1, keepdims=True)


def past_kernel(
    heads, scale, live_ref, q_ref, past_ref, top_ref, total_ref, acc_ref, score_scr, weight_scr
):
    blocks, past_len, _ = past_ref.shape
    for h in range(heads):
        cut = slice(h * HD, (h + 1) * HD)
        v_cut = slice((heads + h) * HD, (heads + h + 1) * HD)
        keys = [past_ref[j, :, cut] for j in range(blocks)]
        top = block_scores(q_ref[:, cut], live_ref, 0, keys, score_scr, scale)
        total = weigh(score_scr, weight_scr, top, blocks)
        values = past_ref[:, :, v_cut].reshape(blocks * past_len, HD)
        acc_ref[:, cut] = jnp.dot(weight_scr[...], values, preferred_element_type=F32)
        top_ref[:, cut] = jnp.broadcast_to(top, (q_ref.shape[0], HD))
        total_ref[:, cut] = jnp.broadcast_to(total, (q_ref.shape[0], HD))


def attend_more(heads, h, scale, live_ref, base, q_ref, kv_ref, running, score_scr, weight_scr):
    chips, tok, _ = kv_ref.shape
    cut = slice(h * HD, (h + 1) * HD)
    v_cut = slice((heads + h) * HD, (heads + h + 1) * HD)
    past_top, past_total, past_acc = [ref[:, cut] for ref in running]
    keys = [kv_ref[j, :, cut] for j in range(chips)]
    top = jnp.maximum(past_top, block_scores(q_ref[:, cut], live_ref, base, keys, score_scr, scale))
    total = weigh(score_scr, weight_scr, top, chips)
    shrink = jnp.exp(past_top - top)
    values = kv_ref[:, :, v_cut].reshape(chips * tok, HD)
    acc = past_acc * shrink + jnp.dot(weight_scr[...], values, preferred_element_type=F32)
    return top, past_total * shrink + total, acc


def near_kernel(
    heads, scale, live_ref, q_ref, near_ref, top_ref, total_ref, acc_ref, top_out, total_out, acc_out, score_scr, weight_scr
):
    running = (top_ref, total_ref, acc_ref)
    for h in range(heads):
        news = attend_more(heads, h, scale, live_ref, 0, q_ref, near_ref, running, score_scr, weight_scr)
        for ref, new in zip((top_out, total_out, acc_out), news):
            ref[:, h * HD : (h + 1) * HD] = new


def far_kernel(
    heads, scale, by_token, live_ref, place_ref, q_ref, far_ref, top_ref, total_ref, acc_ref, w_ref,
    out_ref, score_scr, weight_scr, att_scr,
):
    chips, tok, _ = far_ref.shape
    z = place_ref[0]
    n_z = out_ref.shape[0]
    rows = tok // n_z
    running = (top_ref, total_ref, acc_ref)
    for h in range(heads):
        _, total, acc = attend_more(heads, h, scale, live_ref, chips, q_ref, far_ref, running, score_scr, weight_scr)
        att_scr[:, h * HD : (h + 1) * HD] = (acc / total).astype(BF16)
    full = w_ref.shape[1]
    width = out_ref.shape[2] if not by_token else full // 16
    step = 2 * width
    for c in range(full // step):
        o = jnp.dot(att_scr[...], w_ref[:, c * step : (c + 1) * step], preferred_element_type=F32)
        if by_token:
            o = o.astype(BF16)
            for r in range(n_z):
                out_ref[lax.rem(r + n_z - z, n_z), :, c * step : (c + 1) * step] = o[r * rows : (r + 1) * rows]
        else:
            o = o.T.astype(BF16)
            for half in range(2):
                block = 2 * c + half
                out_ref[lax.rem(block % n_z + n_z - z, n_z), block // n_z] = o[half * width : (half + 1) * width]


def pick_kernel(picked_ref, keys_ref, values_ref, out_ref):
    hw = keys_ref.shape[2]
    for d in range(out_ref.shape[0]):
        out_ref[d, :, :hw] = keys_ref[picked_ref[d]]
        out_ref[d, :, hw:] = values_ref[picked_ref[d]]


def modulate(wide, meansq, mod_ref, cut):
    return (wide * lax.rsqrt(meansq + 1e-06) * (1.0 + mod_ref[1:2, cut]) + mod_ref[0:1, cut]).astype(BF16)


def fetch_weights(w_key_ref, w_value_ref, k_scr, v_scr, sems):
    fetches = [
        pltpu.make_async_copy(w_key_ref, k_scr, sems.at[0]),
        pltpu.make_async_copy(w_value_ref, v_scr, sems.at[1]),
    ]
    for fetch in fetches:
        fetch.start()
    return fetches


def project(normed_scr, weights, fetches, kv_scr, kv_ref, sems):
    for i, (weight, fetch) in enumerate(zip(weights, fetches)):
        fetch.wait()
        width = weight.shape[1]
        out = jnp.dot(normed_scr[...], weight[...], preferred_element_type=F32)
        kv_scr[:, i * width : (i + 1) * width] = out.astype(BF16)
    copies = [pltpu.make_async_copy(kv_scr, kv_ref.at[c], sems.at[4 + c]) for c in range(kv_ref.shape[0])]
    for copy in copies:
        copy.start()
    return copies


def first_norm_kernel(place_ref, mod_ref, w_key_ref, w_value_ref, *refs):
    blocks, (x_out, normed_out, kv_ref, x_ref, normed_ref, turned, k_scr, v_scr, kv_scr, sems) = refs[:-10], refs[-10:]
    fetches = fetch_weights(w_key_ref, w_value_ref, k_scr, v_scr, sems)
    n_z = len(blocks)
    n_yh, width, tok = blocks[0].shape
    full = x_ref.shape[1]
    for k, block in enumerate(blocks):
        here = lax.rem(place_ref[0] + k, n_z)
        for y in range(n_yh):
            row = pl.multiple_of((lax.rem(place_ref[2] + y, n_yh) * n_z + here) * width, 64)
            turned[pl.ds(row, width), :] = block[y]
    squares = jnp.zeros((tok, HD), F32)
    for c in range(full // HD):
        cut = slice(c * HD, (c + 1) * HD)
        wide = turned[cut, :].astype(F32).T
        x_ref[:, cut] = wide.astype(BF16)
        squares = squares + wide * wide
    copies = [pltpu.make_async_copy(x_ref, x_out, sems.at[2])]
    copies[0].start()
    meansq = jnp.sum(squares, axis=1, keepdims=True) * (1.0 / full)
    for c in range(full // HD):
        cut = slice(c * HD, (c + 1) * HD)
        normed_ref[:, cut] = modulate(x_ref[:, cut].astype(F32), meansq, mod_ref, cut)
    copies.append(pltpu.make_async_copy(normed_ref, normed_out, sems.at[3]))
    copies[1].start()
    copies += project(normed_ref, (k_scr, v_scr), fetches, kv_scr, kv_ref, sems)
    for copy in copies:
        copy.wait()


def second_norm_kernel(place_ref, step_ref, mod_ref, x_ref, *refs):
    blocks, (normed_ref, own_ref) = refs[:-2], refs[-2:]
    n_z = len(blocks)
    rows, full = blocks[0].shape
    width = own_ref.shape[1]
    here = place_ref[1] * width
    start = pl.multiple_of(here // HD * HD, HD)
    shift = here - start
    span = -(-width // HD) * HD
    for k, block in enumerate(blocks):
        row = pl.multiple_of(lax.rem(place_ref[0] + k, n_z) * rows, rows)
        squares = jnp.zeros((rows, HD), F32)
        for c in range(full // HD):
            cut = slice(c * HD, (c + 1) * HD)
            x = x_ref[pl.ds(row, rows), cut].astype(F32) + step_ref[0] * block[:, cut].astype(F32)
            x = x.astype(BF16)
            normed_ref[pl.ds(row, rows), cut] = x
            squares = squares + x.astype(F32) * x.astype(F32)
        meansq = jnp.sum(squares, axis=1, keepdims=True) * (1.0 / full)
        for c in range(full // HD):
            cut = slice(c * HD, (c + 1) * HD)
            x = normed_ref[pl.ds(row, rows), cut].astype(F32)
            normed_ref[pl.ds(row, rows), cut] = modulate(x, meansq, mod_ref, cut)
        window = block[:, pl.ds(start, span)].astype(F32)
        window = jnp.where(shift > 0, pltpu.roll(window, span - HD // 2, 1), window)
        own_ref[pl.ds(row, rows), :] = window[:, :width].astype(BF16)


def per_device(
    latent,
    noise_levels,
    mod_table,
    w_query,
    w_key,
    w_value,
    w_out,
    hist_keys,
    hist_values,
    frame_home,
    hist_list,
    list_count,
):
    tok, width = latent.shape
    level_count, _, full = mod_table.shape
    heads = w_query.shape[1] // HD
    hw = heads * HD
    n_ctx = lax.axis_size(CTX)
    n_chip = lax.axis_size(CHIPS)
    n_z = lax.axis_size("z")
    n_yh = lax.axis_size("yh")
    yh = lax.axis_index("yh")
    core = lax.axis_index("core")
    chip = lax.axis_index(CHIPS)
    z = lax.axis_index("z")
    rows = tok // n_z
    scale = 1.0 / math.sqrt(HD)
    down = [(i, (i - 1) % n_z) for i in range(n_z)]
    up = [(i, (i + 1) % n_z) for i in range(n_z)]

    def ring_gather(block, beside):
        got = {0: block}
        for k in range(1, n_z // 2 + 1):
            got[k] = lax.ppermute(got[k - 1], "z", down)
            if 2 * k < n_z:
                got[-k] = lax.ppermute(got[1 - k], "z", up)
            if k == 1 and beside is not None:
                got[1], got[-1], beside = lax.optimization_barrier((got[1], got[-1], beside))
        return [got[k] if 2 * k <= n_z else got[k - n_z] for k in range(n_z)], beside

    def ring_sum(parts):
        low = parts[n_z // 2]
        high = parts[n_z // 2 - 1]
        for k in range(n_z // 2, 0, -1):
            low = lax.ppermute(low, "z", down)
            if 2 * k > 2:
                high = lax.ppermute(high, "z", up)
            low, high = lax.optimization_barrier((low, high))
            if k > 1:
                low = (low.astype(F32) + parts[n_z - k + 1].astype(F32)).astype(BF16)
            if k > 2:
                high = (high.astype(F32) + parts[k - 2].astype(F32)).astype(BF16)
        return parts[0].astype(F32) + low.astype(F32) + high.astype(F32)

    sigma = (noise_levels[:, 0].astype(F32) + 1.0) / level_count
    steps = sigma[1:] - sigma[:-1]

    slot_per_owner, past_len, _ = hist_keys.shape
    frames = jnp.arange(frame_home.shape[0], dtype=jnp.int32)
    wanted = jnp.sum(jnp.where(hist_list[0][:, None] == frames[None, :], frame_home[None, :], 0), axis=1)
    matched = (wanted // slot_per_owner)[:, None] == jnp.arange(n_ctx, dtype=jnp.int32)[None, :]
    request = jnp.sum(jnp.where(matched, (wanted % slot_per_owner)[:, None], 0), axis=0)
    in_list = jnp.arange(n_ctx, dtype=jnp.int32) < list_count[0]
    valid_owner = jnp.any(matched & in_list[:, None], axis=0)
    picked = lax.all_to_all(request[:, None], CTX, split_axis=0, concat_axis=0, tiled=True)[:, 0]
    own = latent.T
    other, picked = lax.optimization_barrier((lax.ppermute(own, "yh", SWAP), picked))
    smem = pl.BlockSpec(memory_space=pltpu.SMEM)
    vmem = pl.BlockSpec(memory_space=pltpu.VMEM)
    hbm = pl.BlockSpec(memory_space=pl.ANY)
    limit = pltpu.CompilerParams(vmem_limit_bytes=24 * 2**20)
    large = pltpu.CompilerParams(vmem_limit_bytes=56 * 2**20)
    asked = pl.pallas_call(
        pick_kernel,
        out_shape=jax.ShapeDtypeStruct((n_ctx, past_len, 2 * hw), BF16),
        in_specs=[smem, vmem, vmem],
        out_specs=vmem,
        compiler_params=large,
    )(picked, hist_keys, hist_values)
    pair = jnp.stack([own, other])
    blocks, asked = ring_gather(pair, asked)
    past = lax.all_to_all(asked, CTX, split_axis=0, concat_axis=0, tiled=True)

    mods = [mod_table[noise_levels[s, 0]] for s in range(2)]
    place = jnp.stack([z, lax.axis_index(TP), yh]).astype(jnp.int32)
    wide = jax.ShapeDtypeStruct((tok, full), BF16)
    kv_copies = jax.ShapeDtypeStruct((n_chip, tok, 2 * hw), BF16)
    wide_scratch = pltpu.VMEM((tok, full), BF16)
    kv_scratch = [
        pltpu.VMEM((full, hw), BF16),
        pltpu.VMEM((full, hw), BF16),
        pltpu.VMEM((tok, 2 * hw), BF16),
        pltpu.SemaphoreType.DMA((4 + n_chip,)),
    ]
    x0_full, normed, kv = pl.pallas_call(
        first_norm_kernel,
        out_shape=[wide, wide, kv_copies],
        in_specs=[smem, vmem, hbm, hbm] + [vmem] * n_z,
        out_specs=[hbm] * 3,
        scratch_shapes=[wide_scratch, wide_scratch, pltpu.VMEM((full, tok), BF16)] + kv_scratch,
        compiler_params=large,
    )(place, mods[0], w_key, w_value, *blocks)

    chips = jnp.arange(n_chip, dtype=jnp.int32)
    seen_own = chips <= chip
    seen_other = (chips < chip) | ((chips == chip) & (core == 1))
    group_live = jnp.concatenate([seen_own, seen_other]).astype(jnp.int32)
    past_live = valid_owner.astype(jnp.int32)

    def attend(normed, kv, past, by_token):
        kv, past = lax.optimization_barrier((kv, past))
        near = lax.all_to_all(kv, CHIPS, split_axis=0, concat_axis=0, tiled=True)
        q = jnp.dot(normed, w_query, preferred_element_type=F32).astype(BF16)
        stat = jax.ShapeDtypeStruct((tok, hw), F32)

        def scratch(keys):
            return [pltpu.VMEM((tok, keys), F32), pltpu.VMEM((tok, keys), BF16)]

        def cost(keys, out):
            return pl.CostEstimate(
                flops=4 * tok * keys * hw + 2 * tok * hw * out,
                bytes_accessed=keys * hw * 4 + hw * out * 2 + tok * out * 2,
                transcendentals=tok * keys * heads,
            )

        past_keys, chip_keys = n_ctx * past_len, n_chip * tok
        top, total, acc = pl.pallas_call(
            functools.partial(past_kernel, heads, scale),
            out_shape=[stat, stat, stat],
            in_specs=[smem] + [vmem] * 2,
            out_specs=[vmem] * 3,
            scratch_shapes=scratch(past_keys),
            compiler_params=limit,
            cost_estimate=cost(past_keys, 0),
        )(past_live, q, past)
        near, top, total, acc = lax.optimization_barrier((near, top, total, acc))
        far = lax.ppermute(near, "core", SWAP)
        top, total, acc = pl.pallas_call(
            functools.partial(near_kernel, heads, scale),
            out_shape=[stat, stat, stat],
            in_specs=[smem] + [vmem] * 5,
            out_specs=[vmem] * 3,
            scratch_shapes=scratch(chip_keys),
            compiler_params=limit,
            cost_estimate=cost(chip_keys, 0),
        )(group_live, q, near, top, total, acc)
        return pl.pallas_call(
            functools.partial(far_kernel, heads, scale, by_token),
            out_shape=jax.ShapeDtypeStruct((n_z, rows, full) if by_token else (n_z, n_yh, width, tok), BF16),
            in_specs=[smem, smem] + [vmem] * 6,
            out_specs=vmem,
            scratch_shapes=scratch(chip_keys) + [pltpu.VMEM((tok, hw), BF16)],
            compiler_params=limit,
            cost_estimate=cost(chip_keys, full),
        )(group_live, place, q, far, top, total, acc, w_out)

    part = attend(normed, kv, past, True)
    half = ring_sum([part[k] for k in range(n_z)]).astype(BF16)
    rest = lax.ppermute(half, "yh", SWAP)
    v0_rows = (half.astype(F32) + rest.astype(F32)).astype(BF16)
    blocks, _ = ring_gather(v0_rows, None)
    normed, v0 = pl.pallas_call(
        second_norm_kernel,
        out_shape=[wide, jax.ShapeDtypeStruct((tok, width), BF16)],
        in_specs=[smem, smem] + [vmem] * (2 + n_z),
        out_specs=[vmem, vmem],
        compiler_params=limit,
    )(place, steps[:1], mods[1], x0_full, *blocks)
    x1 = (latent.astype(F32) + steps[0] * v0.astype(F32)).astype(BF16)

    k = jnp.dot(normed, w_key, preferred_element_type=F32).astype(BF16)
    v = jnp.dot(normed, w_value, preferred_element_type=F32).astype(BF16)
    kv = jnp.broadcast_to(jnp.concatenate([k, v], axis=1)[None], kv_copies.shape)
    part = attend(normed, kv, past, False)
    halves = ring_sum([part[k] for k in range(n_z)]).astype(BF16)
    keep = jnp.where(yh == 1, halves[1], halves[0])
    give = jnp.where(yh == 1, halves[0], halves[1])
    rest = lax.ppermute(give, "yh", SWAP)
    v1 = (keep.astype(F32) + rest.astype(F32)).astype(BF16).T
    x2 = (x1.astype(F32) + steps[1] * v1.astype(F32)).astype(BF16)
    return x2, jnp.stack([v0, v1])


def solution(mesh):
    fine = Mesh(mesh.devices.reshape(2, 4, 2, 2, 8), ("yl", "x", "core", "yh", "z"))
    return jax.shard_map(
        per_device,
        mesh=fine,
        in_specs=(
            P(CTX, TP),
            P(None, CTX),
            P(),
            P(None, TP),
            P(None, TP),
            P(None, TP),
            P(TP, None),
            P(CTX, None, TP),
            P(CTX, None, TP),
            P(),
            P(CTX, None),
            P(CTX),
        ),
        out_specs=(P(CTX, TP), P(None, CTX, TP)),
        check_vma=False,
    )
```

```python
import functools
import math

import jax
import jax.numpy as jnp
from jax import lax
from jax.experimental import pallas as pl
from jax.experimental.pallas import tpu as pltpu
from jax.sharding import Mesh, PartitionSpec as P

HD = 128
CTX = ("yl", "x", "core")
CHIPS = ("yl", "x")
TP = ("yh", "z")
F32, BF16 = jnp.float32, jnp.bfloat16
LOW = -1e30
UNROLL = 4
SWAP = [(0, 1), (1, 0)]


def block_scores(q, live_ref, base, keys, score_scr, scale):
    top = None
    for j, key in enumerate(keys):
        s = lax.dot_general(q, key, (((1,), (1,)), ((), ())), preferred_element_type=F32) * scale
        s = s + jnp.where(live_ref[base + j] > 0, 0.0, LOW)
        score_scr[:, j * HD : (j + 1) * HD] = s
        top = s if top is None else jnp.maximum(top, s)
    return jnp.max(top, axis=1, keepdims=True)


def weigh(score_scr, weight_scr, top, blocks):
    total = None
    for j in range(blocks):
        w = jnp.exp(score_scr[:, j * HD : (j + 1) * HD] - top)
        weight_scr[:, j * HD : (j + 1) * HD] = w.astype(BF16)
        total = w if total is None else total + w
    return jnp.sum(total, axis=1, keepdims=True)


def past_kernel(
    heads, scale, live_ref, q_ref, past_ref, top_ref, total_ref, acc_ref, score_scr, weight_scr
):
    blocks, past_len, _ = past_ref.shape
    for h in range(heads):
        cut = slice(h * HD, (h + 1) * HD)
        v_cut = slice((heads + h) * HD, (heads + h + 1) * HD)
        keys = [past_ref[j, :, cut] for j in range(blocks)]
        top = block_scores(q_ref[:, cut], live_ref, 0, keys, score_scr, scale)
        total = weigh(score_scr, weight_scr, top, blocks)
        values = past_ref[:, :, v_cut].reshape(blocks * past_len, HD)
        acc_ref[:, cut] = jnp.dot(weight_scr[...], values, preferred_element_type=F32)
        top_ref[:, cut] = jnp.broadcast_to(top, (q_ref.shape[0], HD))
        total_ref[:, cut] = jnp.broadcast_to(total, (q_ref.shape[0], HD))


def attend_more(heads, h, scale, live_ref, base, q_ref, kv_ref, running, score_scr, weight_scr):
    chips, tok, _ = kv_ref.shape
    cut = slice(h * HD, (h + 1) * HD)
    v_cut = slice((heads + h) * HD, (heads + h + 1) * HD)
    past_top, past_total, past_acc = [ref[:, cut] for ref in running]
    keys = [kv_ref[j, :, cut] for j in range(chips)]
    top = jnp.maximum(past_top, block_scores(q_ref[:, cut], live_ref, base, keys, score_scr, scale))
    total = weigh(score_scr, weight_scr, top, chips)
    shrink = jnp.exp(past_top - top)
    values = kv_ref[:, :, v_cut].reshape(chips * tok, HD)
    acc = past_acc * shrink + jnp.dot(weight_scr[...], values, preferred_element_type=F32)
    return top, past_total * shrink + total, acc


def near_kernel(
    heads, scale, live_ref, q_ref, near_ref, top_ref, total_ref, acc_ref, top_out, total_out, acc_out, score_scr, weight_scr
):
    running = (top_ref, total_ref, acc_ref)
    for h in range(heads):
        news = attend_more(heads, h, scale, live_ref, 0, q_ref, near_ref, running, score_scr, weight_scr)
        for ref, new in zip((top_out, total_out, acc_out), news):
            ref[:, h * HD : (h + 1) * HD] = new


def far_kernel(
    heads, scale, by_token, live_ref, place_ref, q_ref, far_ref, top_ref, total_ref, acc_ref, w_ref,
    out_ref, score_scr, weight_scr, att_scr,
):
    chips, tok, _ = far_ref.shape
    z = place_ref[0]
    n_z = out_ref.shape[0]
    rows = tok // n_z
    running = (top_ref, total_ref, acc_ref)
    for h in range(heads):
        _, total, acc = attend_more(heads, h, scale, live_ref, chips, q_ref, far_ref, running, score_scr, weight_scr)
        att_scr[:, h * HD : (h + 1) * HD] = (acc / total).astype(BF16)
    full = w_ref.shape[1]
    width = out_ref.shape[2] if not by_token else full // 16
    step = 2 * width
    for c in range(full // step):
        o = jnp.dot(att_scr[...], w_ref[:, c * step : (c + 1) * step], preferred_element_type=F32)
        if by_token:
            o = o.astype(BF16)
            for r in range(n_z):
                out_ref[lax.rem(r + n_z - z, n_z), :, c * step : (c + 1) * step] = o[r * rows : (r + 1) * rows]
        else:
            o = o.T.astype(BF16)
            for half in range(2):
                block = 2 * c + half
                y = lax.rem(block // n_z + place_ref[2], 2)
                out_ref[lax.rem(block % n_z + n_z - z, n_z), y] = o[half * width : (half + 1) * width]


def pick_kernel(picked_ref, keys_ref, values_ref, out_ref):
    hw = keys_ref.shape[2]
    for d in range(out_ref.shape[0]):
        out_ref[d, :, :hw] = keys_ref[picked_ref[d]]
        out_ref[d, :, hw:] = values_ref[picked_ref[d]]


def modulate(wide, meansq, mod_ref, cut):
    return (wide * lax.rsqrt(meansq + 1e-06) * (1.0 + mod_ref[1:2, cut]) + mod_ref[0:1, cut]).astype(BF16)


def fetch_weights(w_key_ref, w_value_ref, k_scr, v_scr, sems):
    fetches = [
        pltpu.make_async_copy(w_key_ref, k_scr, sems.at[0]),
        pltpu.make_async_copy(w_value_ref, v_scr, sems.at[1]),
    ]
    for fetch in fetches:
        fetch.start()
    return fetches


def project(normed_scr, weights, fetches, kv_scr, kv_ref, sems):
    for i, (weight, fetch) in enumerate(zip(weights, fetches)):
        fetch.wait()
        width = weight.shape[1]
        out = jnp.dot(normed_scr[...], weight[...], preferred_element_type=F32)
        kv_scr[:, i * width : (i + 1) * width] = out.astype(BF16)
    copies = [pltpu.make_async_copy(kv_scr, kv_ref.at[c], sems.at[4 + c]) for c in range(kv_ref.shape[0])]
    for copy in copies:
        copy.start()
    return copies


def first_norm_kernel(place_ref, mod_ref, w_key_ref, w_value_ref, *refs):
    blocks, (x_out, normed_out, kv_ref, x_ref, normed_ref, turned, k_scr, v_scr, kv_scr, sems) = refs[:-10], refs[-10:]
    fetches = fetch_weights(w_key_ref, w_value_ref, k_scr, v_scr, sems)
    n_z = len(blocks)
    n_yh, width, tok = blocks[0].shape
    full = x_ref.shape[1]
    for k, block in enumerate(blocks):
        here = lax.rem(place_ref[0] + k, n_z)
        for y in range(n_yh):
            row = pl.multiple_of((lax.rem(place_ref[2] + y, n_yh) * n_z + here) * width, 64)
            turned[pl.ds(row, width), :] = block[y]
    def turn(c, squares):
        cut = pl.ds(pl.multiple_of(c * HD, HD), HD)
        wide = turned[cut, :].astype(F32).T
        x_ref[:, cut] = wide.astype(BF16)
        return squares + wide * wide

    squares = lax.fori_loop(0, full // HD, turn, jnp.zeros((tok, HD), F32), unroll=UNROLL)
    copies = [pltpu.make_async_copy(x_ref, x_out, sems.at[2])]
    copies[0].start()
    meansq = jnp.sum(squares, axis=1, keepdims=True) * (1.0 / full)
    def apply(c, _):
        cut = pl.ds(pl.multiple_of(c * HD, HD), HD)
        normed_ref[:, cut] = modulate(x_ref[:, cut].astype(F32), meansq, mod_ref, cut)
        return 0

    lax.fori_loop(0, full // HD, apply, 0, unroll=UNROLL)
    copies.append(pltpu.make_async_copy(normed_ref, normed_out, sems.at[3]))
    copies[1].start()
    copies += project(normed_ref, (k_scr, v_scr), fetches, kv_scr, kv_ref, sems)
    for copy in copies:
        copy.wait()


def second_norm_kernel(place_ref, step_ref, mod_ref, x_ref, *refs):
    blocks, (normed_ref, own_ref) = refs[:-2], refs[-2:]
    n_z = len(blocks)
    rows, full = blocks[0].shape
    width = own_ref.shape[1]
    here = place_ref[1] * width
    start = pl.multiple_of(here // HD * HD, HD)
    shift = here - start
    span = -(-width // HD) * HD
    for k, block in enumerate(blocks):
        row = pl.multiple_of(lax.rem(place_ref[0] + k, n_z) * rows, rows)
        squares = jnp.zeros((rows, HD), F32)
        for c in range(full // HD):
            cut = slice(c * HD, (c + 1) * HD)
            x = x_ref[pl.ds(row, rows), cut].astype(F32) + step_ref[0] * block[:, cut].astype(F32)
            x = x.astype(BF16)
            normed_ref[pl.ds(row, rows), cut] = x
            squares = squares + x.astype(F32) * x.astype(F32)
        meansq = jnp.sum(squares, axis=1, keepdims=True) * (1.0 / full)
        for c in range(full // HD):
            cut = slice(c * HD, (c + 1) * HD)
            x = normed_ref[pl.ds(row, rows), cut].astype(F32)
            normed_ref[pl.ds(row, rows), cut] = modulate(x, meansq, mod_ref, cut)
        window = block[:, pl.ds(start, span)].astype(F32)
        window = jnp.where(shift > 0, pltpu.roll(window, span - HD // 2, 1), window)
        own_ref[pl.ds(row, rows), :] = window[:, :width].astype(BF16)


def per_device(
    latent,
    noise_levels,
    mod_table,
    w_query,
    w_key,
    w_value,
    w_out,
    hist_keys,
    hist_values,
    frame_home,
    hist_list,
    list_count,
):
    tok, width = latent.shape
    level_count, _, full = mod_table.shape
    heads = w_query.shape[1] // HD
    hw = heads * HD
    n_ctx = lax.axis_size(CTX)
    n_chip = lax.axis_size(CHIPS)
    n_z = lax.axis_size("z")
    n_yh = lax.axis_size("yh")
    yh = lax.axis_index("yh")
    core = lax.axis_index("core")
    chip = lax.axis_index(CHIPS)
    z = lax.axis_index("z")
    rows = tok // n_z
    scale = 1.0 / math.sqrt(HD)
    down = [(i, (i - 1) % n_z) for i in range(n_z)]
    up = [(i, (i + 1) % n_z) for i in range(n_z)]

    def ring_gather(block, beside):
        got = {0: block}
        for k in range(1, n_z // 2 + 1):
            got[k] = lax.ppermute(got[k - 1], "z", down)
            if 2 * k < n_z:
                got[-k] = lax.ppermute(got[1 - k], "z", up)
            if k == 1 and beside is not None:
                got[1], got[-1], beside = lax.optimization_barrier((got[1], got[-1], beside))
        return [got[k] if 2 * k <= n_z else got[k - n_z] for k in range(n_z)], beside

    cross = [(i, (i + n_z) % (n_yh * n_z)) for i in range(n_yh * n_z)]
    cross_down = [(y * n_z + a, (1 - y) * n_z + b) for y in range(n_yh) for a, b in down]

    def add(a, b):
        return (a.astype(F32) + b.astype(F32)).astype(BF16)

    def ring_sum(parts):
        low = parts[n_z // 2]
        high = parts[n_z // 2 - 1]
        for k in range(n_z // 2 - 1, 0, -1):
            low = lax.ppermute(low, "z", down)
            high = lax.ppermute(high, "z", up)
            low, high = lax.optimization_barrier((low, high))
            low = add(low, parts[n_z - k])
            high = add(high, parts[k - 1])
        return high, low

    sigma = (noise_levels[:, 0].astype(F32) + 1.0) / level_count
    steps = sigma[1:] - sigma[:-1]

    slot_per_owner, past_len, _ = hist_keys.shape
    frames = jnp.arange(frame_home.shape[0], dtype=jnp.int32)
    wanted = jnp.sum(jnp.where(hist_list[0][:, None] == frames[None, :], frame_home[None, :], 0), axis=1)
    matched = (wanted // slot_per_owner)[:, None] == jnp.arange(n_ctx, dtype=jnp.int32)[None, :]
    request = jnp.sum(jnp.where(matched, (wanted % slot_per_owner)[:, None], 0), axis=0)
    in_list = jnp.arange(n_ctx, dtype=jnp.int32) < list_count[0]
    valid_owner = jnp.any(matched & in_list[:, None], axis=0)
    picked = lax.all_to_all(request[:, None], CTX, split_axis=0, concat_axis=0, tiled=True)[:, 0]
    own = latent.T
    other, picked = lax.optimization_barrier((lax.ppermute(own, "yh", SWAP), picked))
    smem = pl.BlockSpec(memory_space=pltpu.SMEM)
    vmem = pl.BlockSpec(memory_space=pltpu.VMEM)
    hbm = pl.BlockSpec(memory_space=pl.ANY)
    limit = pltpu.CompilerParams(vmem_limit_bytes=24 * 2**20)
    large = pltpu.CompilerParams(vmem_limit_bytes=56 * 2**20)
    asked = pl.pallas_call(
        pick_kernel,
        out_shape=jax.ShapeDtypeStruct((n_ctx, past_len, 2 * hw), BF16),
        in_specs=[smem, vmem, vmem],
        out_specs=vmem,
        compiler_params=large,
    )(picked, hist_keys, hist_values)
    pair = jnp.stack([own, other])
    blocks, asked = ring_gather(pair, asked)
    past = lax.all_to_all(asked, CTX, split_axis=0, concat_axis=0, tiled=True)

    mods = [mod_table[noise_levels[s, 0]] for s in range(2)]
    place = jnp.stack([z, lax.axis_index(TP), yh]).astype(jnp.int32)
    wide = jax.ShapeDtypeStruct((tok, full), BF16)
    kv_copies = jax.ShapeDtypeStruct((n_chip, tok, 2 * hw), BF16)
    wide_scratch = pltpu.VMEM((tok, full), BF16)
    kv_scratch = [
        pltpu.VMEM((full, hw), BF16),
        pltpu.VMEM((full, hw), BF16),
        pltpu.VMEM((tok, 2 * hw), BF16),
        pltpu.SemaphoreType.DMA((4 + n_chip,)),
    ]
    x0_full, normed, kv = pl.pallas_call(
        first_norm_kernel,
        out_shape=[wide, wide, kv_copies],
        in_specs=[smem, vmem, hbm, hbm] + [vmem] * n_z,
        out_specs=[hbm] * 3,
        scratch_shapes=[wide_scratch, wide_scratch, pltpu.VMEM((full, tok), BF16)] + kv_scratch,
        compiler_params=large,
    )(place, mods[0], w_key, w_value, *blocks)

    chips = jnp.arange(n_chip, dtype=jnp.int32)
    seen_own = chips <= chip
    seen_other = (chips < chip) | ((chips == chip) & (core == 1))
    group_live = jnp.concatenate([seen_own, seen_other]).astype(jnp.int32)
    past_live = valid_owner.astype(jnp.int32)

    def attend(normed, kv, past, by_token):
        kv, past = lax.optimization_barrier((kv, past))
        near = lax.all_to_all(kv, CHIPS, split_axis=0, concat_axis=0, tiled=True)
        q = jnp.dot(normed, w_query, preferred_element_type=F32).astype(BF16)
        stat = jax.ShapeDtypeStruct((tok, hw), F32)

        def scratch(keys):
            return [pltpu.VMEM((tok, keys), F32), pltpu.VMEM((tok, keys), BF16)]

        def cost(keys, out):
            return pl.CostEstimate(
                flops=4 * tok * keys * hw + 2 * tok * hw * out,
                bytes_accessed=8 * keys * hw * 4 + hw * out * 2 + tok * out * 2,
                transcendentals=tok * keys * heads,
            )

        past_keys, chip_keys = n_ctx * past_len, n_chip * tok
        top, total, acc = pl.pallas_call(
            functools.partial(past_kernel, heads, scale),
            out_shape=[stat, stat, stat],
            in_specs=[smem] + [vmem] * 2,
            out_specs=[vmem] * 3,
            scratch_shapes=scratch(past_keys),
            compiler_params=limit,
            cost_estimate=cost(past_keys, 0),
        )(past_live, q, past)
        near, top, total, acc = lax.optimization_barrier((near, top, total, acc))
        far = lax.ppermute(near, "core", SWAP)
        top, total, acc = pl.pallas_call(
            functools.partial(near_kernel, heads, scale),
            out_shape=[stat, stat, stat],
            in_specs=[smem] + [vmem] * 5,
            out_specs=[vmem] * 3,
            scratch_shapes=scratch(chip_keys),
            compiler_params=limit,
            cost_estimate=cost(chip_keys, 0),
        )(group_live, q, near, top, total, acc)
        return pl.pallas_call(
            functools.partial(far_kernel, heads, scale, by_token),
            out_shape=jax.ShapeDtypeStruct((n_z, rows, full) if by_token else (n_z, n_yh, width, tok), BF16),
            in_specs=[smem, smem] + [vmem] * 6,
            out_specs=vmem,
            scratch_shapes=scratch(chip_keys) + [pltpu.VMEM((tok, hw), BF16)],
            compiler_params=limit,
            cost_estimate=cost(chip_keys, full),
        )(group_live, place, q, far, top, total, acc, w_out)

    part = attend(normed, kv, past, True)
    high, low = ring_sum([part[k] for k in range(n_z)])
    here = (high, lax.ppermute(low, "z", down))
    there = (lax.ppermute(high, TP, cross), lax.ppermute(low, TP, cross_down))
    here, there = [a.astype(F32) + b.astype(F32) for a, b in (here, there)]
    v0_rows = (here + there).astype(BF16)
    blocks, _ = ring_gather(v0_rows, None)
    normed, v0 = pl.pallas_call(
        second_norm_kernel,
        out_shape=[wide, jax.ShapeDtypeStruct((tok, width), BF16)],
        in_specs=[smem, smem] + [vmem] * (2 + n_z),
        out_specs=[vmem, vmem],
        compiler_params=limit,
        cost_estimate=pl.CostEstimate(flops=16 * tok * full, bytes_accessed=24 * 2**20, transcendentals=tok),
    )(place, steps[:1], mods[1], x0_full, *blocks)
    x1 = (latent.astype(F32) + steps[0] * v0.astype(F32)).astype(BF16)

    k = jnp.dot(normed, w_key, preferred_element_type=F32).astype(BF16)
    v = jnp.dot(normed, w_value, preferred_element_type=F32).astype(BF16)
    kv = jnp.broadcast_to(jnp.concatenate([k, v], axis=1)[None], kv_copies.shape)
    part = attend(normed, kv, past, False)
    high, low = ring_sum([part[k] for k in range(n_z)])
    here = (high[0], lax.ppermute(low[0], "z", down))
    there = (lax.ppermute(high[1], TP, cross), lax.ppermute(low[1], TP, cross_down))
    v1 = sum(x.astype(F32) for x in here + there).astype(BF16).T
    x2 = (x1.astype(F32) + steps[1] * v1.astype(F32)).astype(BF16)
    return x2, jnp.stack([v0, v1])


def solution(mesh):
    fine = Mesh(mesh.devices.reshape(2, 4, 2, 2, 8), ("yl", "x", "core", "yh", "z"))
    return jax.shard_map(
        per_device,
        mesh=fine,
        in_specs=(
            P(CTX, TP),
            P(None, CTX),
            P(),
            P(None, TP),
            P(None, TP),
            P(None, TP),
            P(TP, None),
            P(CTX, None, TP),
            P(CTX, None, TP),
            P(),
            P(CTX, None),
            P(CTX),
        ),
        out_specs=(P(CTX, TP), P(None, CTX, TP)),
        check_vma=False,
    )
```

```python
import functools
import math

import jax
import jax.numpy as jnp
from jax import lax
from jax.experimental import pallas as pl
from jax.experimental.pallas import tpu as pltpu
from jax.sharding import Mesh, PartitionSpec as P

HD = 128
CTX = ("yl", "x", "core")
CHIPS = ("yl", "x")
TP = ("yh", "z")
F32, BF16 = jnp.float32, jnp.bfloat16
LOW = -1e30
UNROLL = 4
SWAP = [(0, 1), (1, 0)]


def block_scores(q, live_ref, base, keys, score_scr, scale):
    top = None
    for j, key in enumerate(keys):
        s = lax.dot_general(q, key, (((1,), (1,)), ((), ())), preferred_element_type=F32) * scale
        s = s + jnp.where(live_ref[base + j] > 0, 0.0, LOW)
        score_scr[:, j * HD : (j + 1) * HD] = s
        top = s if top is None else jnp.maximum(top, s)
    return jnp.max(top, axis=1, keepdims=True)


def weigh(score_scr, weight_scr, top, blocks):
    total = None
    for j in range(blocks):
        w = jnp.exp(score_scr[:, j * HD : (j + 1) * HD] - top)
        weight_scr[:, j * HD : (j + 1) * HD] = w.astype(BF16)
        total = w if total is None else total + w
    return jnp.sum(total, axis=1, keepdims=True)


def past_kernel(
    heads, scale, live_ref, q_ref, past_ref, top_ref, total_ref, acc_ref, score_scr, weight_scr
):
    blocks, past_len, _ = past_ref.shape
    for h in range(heads):
        cut = slice(h * HD, (h + 1) * HD)
        v_cut = slice((heads + h) * HD, (heads + h + 1) * HD)
        keys = [past_ref[j, :, cut] for j in range(blocks)]
        top = block_scores(q_ref[:, cut], live_ref, 0, keys, score_scr, scale)
        total = weigh(score_scr, weight_scr, top, blocks)
        values = past_ref[:, :, v_cut].reshape(blocks * past_len, HD)
        acc_ref[:, cut] = jnp.dot(weight_scr[...], values, preferred_element_type=F32)
        top_ref[:, cut] = jnp.broadcast_to(top, (q_ref.shape[0], HD))
        total_ref[:, cut] = jnp.broadcast_to(total, (q_ref.shape[0], HD))


def attend_more(heads, h, scale, live_ref, base, q_ref, kv_ref, running, score_scr, weight_scr):
    chips, tok, _ = kv_ref.shape
    cut = slice(h * HD, (h + 1) * HD)
    v_cut = slice((heads + h) * HD, (heads + h + 1) * HD)
    past_top, past_total, past_acc = [ref[:, cut] for ref in running]
    keys = [kv_ref[j, :, cut] for j in range(chips)]
    top = jnp.maximum(past_top, block_scores(q_ref[:, cut], live_ref, base, keys, score_scr, scale))
    total = weigh(score_scr, weight_scr, top, chips)
    shrink = jnp.exp(past_top - top)
    values = kv_ref[:, :, v_cut].reshape(chips * tok, HD)
    acc = past_acc * shrink + jnp.dot(weight_scr[...], values, preferred_element_type=F32)
    return top, past_total * shrink + total, acc


def near_kernel(
    heads, scale, live_ref, q_ref, near_ref, top_ref, total_ref, acc_ref, top_out, total_out, acc_out, score_scr, weight_scr
):
    running = (top_ref, total_ref, acc_ref)
    for h in range(heads):
        news = attend_more(heads, h, scale, live_ref, 0, q_ref, near_ref, running, score_scr, weight_scr)
        for ref, new in zip((top_out, total_out, acc_out), news):
            ref[:, h * HD : (h + 1) * HD] = new


def far_kernel(
    heads, scale, by_token, live_ref, place_ref, q_ref, far_ref, top_ref, total_ref, acc_ref, w_ref,
    out_ref, score_scr, weight_scr, att_scr,
):
    chips, tok, _ = far_ref.shape
    z = place_ref[0]
    n_z = out_ref.shape[0]
    rows = tok // n_z
    running = (top_ref, total_ref, acc_ref)
    for h in range(heads):
        _, total, acc = attend_more(heads, h, scale, live_ref, chips, q_ref, far_ref, running, score_scr, weight_scr)
        att_scr[:, h * HD : (h + 1) * HD] = (acc / total).astype(BF16)
    full = w_ref.shape[1]
    width = out_ref.shape[2] if not by_token else full // 16
    step = 2 * width
    for c in range(full // step):
        o = jnp.dot(att_scr[...], w_ref[:, c * step : (c + 1) * step], preferred_element_type=F32)
        if by_token:
            for r in range(n_z):
                out_ref[lax.rem(r + n_z - z, n_z), :, c * step : (c + 1) * step] = o[r * rows : (r + 1) * rows]
        else:
            o = o.T
            for half in range(2):
                block = 2 * c + half
                out_ref[lax.rem(block % n_z + n_z - z, n_z), block // n_z] = o[half * width : (half + 1) * width]


def pick_kernel(picked_ref, keys_ref, values_ref, out_ref):
    hw = keys_ref.shape[2]
    for d in range(out_ref.shape[0]):
        out_ref[d, :, :hw] = keys_ref[picked_ref[d]]
        out_ref[d, :, hw:] = values_ref[picked_ref[d]]


def modulate(wide, meansq, mod_ref, cut):
    return (wide * lax.rsqrt(meansq + 1e-06) * (1.0 + mod_ref[1:2, cut]) + mod_ref[0:1, cut]).astype(BF16)


def fetch_weights(w_key_ref, w_value_ref, k_scr, v_scr, sems):
    fetches = [
        pltpu.make_async_copy(w_key_ref, k_scr, sems.at[0]),
        pltpu.make_async_copy(w_value_ref, v_scr, sems.at[1]),
    ]
    for fetch in fetches:
        fetch.start()
    return fetches


def project(normed_scr, weights, fetches, kv_scr, kv_ref, sems):
    for i, (weight, fetch) in enumerate(zip(weights, fetches)):
        fetch.wait()
        width = weight.shape[1]
        out = jnp.dot(normed_scr[...], weight[...], preferred_element_type=F32)
        kv_scr[:, i * width : (i + 1) * width] = out.astype(BF16)
    copies = [pltpu.make_async_copy(kv_scr, kv_ref.at[c], sems.at[4 + c]) for c in range(kv_ref.shape[0])]
    for copy in copies:
        copy.start()
    return copies


def first_norm_kernel(place_ref, mod_ref, w_key_ref, w_value_ref, *refs):
    blocks, (x_out, normed_out, kv_ref, x_ref, normed_ref, turned, k_scr, v_scr, kv_scr, sems) = refs[:-10], refs[-10:]
    fetches = fetch_weights(w_key_ref, w_value_ref, k_scr, v_scr, sems)
    n_z = len(blocks)
    n_yh, width, tok = blocks[0].shape
    full = x_ref.shape[1]
    for k, block in enumerate(blocks):
        here = lax.rem(place_ref[0] + k, n_z)
        for y in range(n_yh):
            row = pl.multiple_of((lax.rem(place_ref[2] + y, n_yh) * n_z + here) * width, 64)
            turned[pl.ds(row, width), :] = block[y]
    def turn(c, squares):
        cut = pl.ds(pl.multiple_of(c * HD, HD), HD)
        wide = turned[cut, :].astype(F32).T
        x_ref[:, cut] = wide.astype(BF16)
        return squares + wide * wide

    squares = lax.fori_loop(0, full // HD, turn, jnp.zeros((tok, HD), F32), unroll=UNROLL)
    copies = [pltpu.make_async_copy(x_ref, x_out, sems.at[2])]
    copies[0].start()
    meansq = jnp.sum(squares, axis=1, keepdims=True) * (1.0 / full)
    def apply(c, _):
        cut = pl.ds(pl.multiple_of(c * HD, HD), HD)
        normed_ref[:, cut] = modulate(x_ref[:, cut].astype(F32), meansq, mod_ref, cut)
        return 0

    lax.fori_loop(0, full // HD, apply, 0, unroll=UNROLL)
    copies.append(pltpu.make_async_copy(normed_ref, normed_out, sems.at[3]))
    copies[1].start()
    copies += project(normed_ref, (k_scr, v_scr), fetches, kv_scr, kv_ref, sems)
    for copy in copies:
        copy.wait()


def second_norm_kernel(place_ref, step_ref, mod_ref, x_ref, *refs):
    blocks, (normed_ref, own_ref) = refs[:-2], refs[-2:]
    n_z = len(blocks)
    rows, full = blocks[0].shape
    width = own_ref.shape[1]
    here = place_ref[1] * width
    start = pl.multiple_of(here // HD * HD, HD)
    shift = here - start
    span = -(-width // HD) * HD
    for k, block in enumerate(blocks):
        row = pl.multiple_of(lax.rem(place_ref[0] + k, n_z) * rows, rows)
        squares = jnp.zeros((rows, HD), F32)
        for c in range(full // HD):
            cut = slice(c * HD, (c + 1) * HD)
            x = x_ref[pl.ds(row, rows), cut].astype(F32) + step_ref[0] * block[:, cut].astype(F32)
            x = x.astype(BF16)
            normed_ref[pl.ds(row, rows), cut] = x
            squares = squares + x.astype(F32) * x.astype(F32)
        meansq = jnp.sum(squares, axis=1, keepdims=True) * (1.0 / full)
        for c in range(full // HD):
            cut = slice(c * HD, (c + 1) * HD)
            x = normed_ref[pl.ds(row, rows), cut].astype(F32)
            normed_ref[pl.ds(row, rows), cut] = modulate(x, meansq, mod_ref, cut)
        window = block[:, pl.ds(start, span)].astype(F32)
        window = jnp.where(shift > 0, pltpu.roll(window, span - HD // 2, 1), window)
        own_ref[pl.ds(row, rows), :] = window[:, :width].astype(BF16)


def per_device(
    latent,
    noise_levels,
    mod_table,
    w_query,
    w_key,
    w_value,
    w_out,
    hist_keys,
    hist_values,
    frame_home,
    hist_list,
    list_count,
):
    tok, width = latent.shape
    level_count, _, full = mod_table.shape
    heads = w_query.shape[1] // HD
    hw = heads * HD
    n_ctx = lax.axis_size(CTX)
    n_chip = lax.axis_size(CHIPS)
    n_z = lax.axis_size("z")
    n_yh = lax.axis_size("yh")
    yh = lax.axis_index("yh")
    core = lax.axis_index("core")
    chip = lax.axis_index(CHIPS)
    z = lax.axis_index("z")
    rows = tok // n_z
    scale = 1.0 / math.sqrt(HD)
    down = [(i, (i - 1) % n_z) for i in range(n_z)]
    up = [(i, (i + 1) % n_z) for i in range(n_z)]

    def ring_gather(block, beside):
        got = {0: block}
        for k in range(1, n_z // 2 + 1):
            got[k] = lax.ppermute(got[k - 1], "z", down)
            if 2 * k < n_z:
                got[-k] = lax.ppermute(got[1 - k], "z", up)
            if k == 1 and beside is not None:
                got[1], got[-1], beside = lax.optimization_barrier((got[1], got[-1], beside))
        return [got[k] if 2 * k <= n_z else got[k - n_z] for k in range(n_z)], beside

    def ring_sum(parts):
        low = parts[n_z // 2]
        high = parts[n_z // 2 - 1]
        for k in range(n_z // 2, 0, -1):
            low = lax.ppermute(low, "z", down)
            if 2 * k > 2:
                high = lax.ppermute(high, "z", up)
            low, high = lax.optimization_barrier((low, high))
            if k > 1:
                low = low + parts[n_z - k + 1]
            if k > 2:
                high = high + parts[k - 2]
        return parts[0] + low + high

    sigma = (noise_levels[:, 0].astype(F32) + 1.0) / level_count
    steps = sigma[1:] - sigma[:-1]

    slot_per_owner, past_len, _ = hist_keys.shape
    frames = jnp.arange(frame_home.shape[0], dtype=jnp.int32)
    wanted = jnp.sum(jnp.where(hist_list[0][:, None] == frames[None, :], frame_home[None, :], 0), axis=1)
    matched = (wanted // slot_per_owner)[:, None] == jnp.arange(n_ctx, dtype=jnp.int32)[None, :]
    request = jnp.sum(jnp.where(matched, (wanted % slot_per_owner)[:, None], 0), axis=0)
    in_list = jnp.arange(n_ctx, dtype=jnp.int32) < list_count[0]
    valid_owner = jnp.any(matched & in_list[:, None], axis=0)
    picked = lax.all_to_all(request[:, None], CTX, split_axis=0, concat_axis=0, tiled=True)[:, 0]
    own = latent.T
    other, picked = lax.optimization_barrier((lax.ppermute(own, "yh", SWAP), picked))
    smem = pl.BlockSpec(memory_space=pltpu.SMEM)
    vmem = pl.BlockSpec(memory_space=pltpu.VMEM)
    hbm = pl.BlockSpec(memory_space=pl.ANY)
    limit = pltpu.CompilerParams(vmem_limit_bytes=24 * 2**20)
    large = pltpu.CompilerParams(vmem_limit_bytes=56 * 2**20)
    asked = pl.pallas_call(
        pick_kernel,
        out_shape=jax.ShapeDtypeStruct((n_ctx, past_len, 2 * hw), BF16),
        in_specs=[smem, vmem, vmem],
        out_specs=vmem,
        compiler_params=large,
    )(picked, hist_keys, hist_values)
    pair = jnp.stack([own, other])
    blocks, asked = ring_gather(pair, asked)
    past = lax.all_to_all(asked, CTX, split_axis=0, concat_axis=0, tiled=True)

    mods = [mod_table[noise_levels[s, 0]] for s in range(2)]
    place = jnp.stack([z, lax.axis_index(TP), yh]).astype(jnp.int32)
    wide = jax.ShapeDtypeStruct((tok, full), BF16)
    kv_copies = jax.ShapeDtypeStruct((n_chip, tok, 2 * hw), BF16)
    wide_scratch = pltpu.VMEM((tok, full), BF16)
    kv_scratch = [
        pltpu.VMEM((full, hw), BF16),
        pltpu.VMEM((full, hw), BF16),
        pltpu.VMEM((tok, 2 * hw), BF16),
        pltpu.SemaphoreType.DMA((4 + n_chip,)),
    ]
    x0_full, normed, kv = pl.pallas_call(
        first_norm_kernel,
        out_shape=[wide, wide, kv_copies],
        in_specs=[smem, vmem, hbm, hbm] + [vmem] * n_z,
        out_specs=[hbm] * 3,
        scratch_shapes=[wide_scratch, wide_scratch, pltpu.VMEM((full, tok), BF16)] + kv_scratch,
        compiler_params=large,
    )(place, mods[0], w_key, w_value, *blocks)

    chips = jnp.arange(n_chip, dtype=jnp.int32)
    seen_own = chips <= chip
    seen_other = (chips < chip) | ((chips == chip) & (core == 1))
    group_live = jnp.concatenate([seen_own, seen_other]).astype(jnp.int32)
    past_live = valid_owner.astype(jnp.int32)

    def attend(normed, kv, past, by_token):
        kv, past = lax.optimization_barrier((kv, past))
        near = lax.all_to_all(kv, CHIPS, split_axis=0, concat_axis=0, tiled=True)
        q = jnp.dot(normed, w_query, preferred_element_type=F32).astype(BF16)
        stat = jax.ShapeDtypeStruct((tok, hw), F32)

        def scratch(keys):
            return [pltpu.VMEM((tok, keys), F32), pltpu.VMEM((tok, keys), BF16)]

        def cost(keys, out):
            return pl.CostEstimate(
                flops=4 * tok * keys * hw + 2 * tok * hw * out,
                bytes_accessed=8 * keys * hw * 4 + hw * out * 2 + tok * out * 2,
                transcendentals=tok * keys * heads,
            )

        past_keys, chip_keys = n_ctx * past_len, n_chip * tok
        top, total, acc = pl.pallas_call(
            functools.partial(past_kernel, heads, scale),
            out_shape=[stat, stat, stat],
            in_specs=[smem] + [vmem] * 2,
            out_specs=[vmem] * 3,
            scratch_shapes=scratch(past_keys),
            compiler_params=limit,
            cost_estimate=cost(past_keys, 0),
        )(past_live, q, past)
        near, top, total, acc = lax.optimization_barrier((near, top, total, acc))
        far = lax.ppermute(near, "core", SWAP)
        top, total, acc = pl.pallas_call(
            functools.partial(near_kernel, heads, scale),
            out_shape=[stat, stat, stat],
            in_specs=[smem] + [vmem] * 5,
            out_specs=[vmem] * 3,
            scratch_shapes=scratch(chip_keys),
            compiler_params=limit,
            cost_estimate=cost(chip_keys, 0),
        )(group_live, q, near, top, total, acc)
        return pl.pallas_call(
            functools.partial(far_kernel, heads, scale, by_token),
            out_shape=jax.ShapeDtypeStruct((n_z, rows, full) if by_token else (n_z, n_yh, width, tok), F32),
            in_specs=[smem, smem] + [vmem] * 6,
            out_specs=vmem,
            scratch_shapes=scratch(chip_keys) + [pltpu.VMEM((tok, hw), BF16)],
            compiler_params=limit,
            cost_estimate=cost(chip_keys, full),
        )(group_live, place, q, far, top, total, acc, w_out)

    part = attend(normed, kv, past, True)
    half = ring_sum([part[k] for k in range(n_z)])
    rest = lax.ppermute(half, "yh", SWAP)
    v0_rows = (half + rest).astype(BF16)
    blocks, _ = ring_gather(v0_rows, None)
    normed, v0 = pl.pallas_call(
        second_norm_kernel,
        out_shape=[wide, jax.ShapeDtypeStruct((tok, width), BF16)],
        in_specs=[smem, smem] + [vmem] * (2 + n_z),
        out_specs=[vmem, vmem],
        compiler_params=limit,
        cost_estimate=pl.CostEstimate(flops=16 * tok * full, bytes_accessed=24 * 2**20, transcendentals=tok),
    )(place, steps[:1], mods[1], x0_full, *blocks)
    x1 = (latent.astype(F32) + steps[0] * v0.astype(F32)).astype(BF16)

    k = jnp.dot(normed, w_key, preferred_element_type=F32).astype(BF16)
    v = jnp.dot(normed, w_value, preferred_element_type=F32).astype(BF16)
    kv = jnp.broadcast_to(jnp.concatenate([k, v], axis=1)[None], kv_copies.shape)
    part = attend(normed, kv, past, False)
    halves = ring_sum([part[k] for k in range(n_z)])
    keep = jnp.where(yh == 1, halves[1], halves[0])
    give = jnp.where(yh == 1, halves[0], halves[1])
    rest = lax.ppermute(give, "yh", SWAP)
    v1 = (keep + rest).astype(BF16).T
    x2 = (x1.astype(F32) + steps[1] * v1.astype(F32)).astype(BF16)
    return x2, jnp.stack([v0, v1])


def solution(mesh):
    fine = Mesh(mesh.devices.reshape(2, 4, 2, 2, 8), ("yl", "x", "core", "yh", "z"))
    return jax.shard_map(
        per_device,
        mesh=fine,
        in_specs=(
            P(CTX, TP),
            P(None, CTX),
            P(),
            P(None, TP),
            P(None, TP),
            P(None, TP),
            P(TP, None),
            P(CTX, None, TP),
            P(CTX, None, TP),
            P(),
            P(CTX, None),
            P(CTX),
        ),
        out_specs=(P(CTX, TP), P(None, CTX, TP)),
        check_vma=False,
    )
```

```python
import functools
import math

import jax
import jax.numpy as jnp
from jax import lax
from jax.experimental import pallas as pl
from jax.experimental.pallas import tpu as pltpu
from jax.sharding import Mesh, PartitionSpec as P

HD = 128
CTX = ("yl", "x", "core")
CHIPS = ("yl", "x")
TP = ("yh", "z")
F32, BF16 = jnp.float32, jnp.bfloat16
LOW = -1e30
UNROLL = 4
SWAP = [(0, 1), (1, 0)]


def block_scores(q, live_ref, base, keys, score_scr, scale):
    top = None
    for j, key in enumerate(keys):
        s = lax.dot_general(q, key, (((1,), (1,)), ((), ())), preferred_element_type=F32) * scale
        s = s + jnp.where(live_ref[base + j] > 0, 0.0, LOW)
        score_scr[:, j * HD : (j + 1) * HD] = s
        top = s if top is None else jnp.maximum(top, s)
    return jnp.max(top, axis=1, keepdims=True)


def weigh(score_scr, weight_scr, top, blocks):
    total = None
    for j in range(blocks):
        w = jnp.exp(score_scr[:, j * HD : (j + 1) * HD] - top)
        weight_scr[:, j * HD : (j + 1) * HD] = w.astype(BF16)
        total = w if total is None else total + w
    return jnp.sum(total, axis=1, keepdims=True)


def past_kernel(
    heads, scale, live_ref, q_ref, past_ref, top_ref, total_ref, acc_ref, score_scr, weight_scr
):
    blocks, past_len, _ = past_ref.shape
    for h in range(heads):
        cut = slice(h * HD, (h + 1) * HD)
        v_cut = slice((heads + h) * HD, (heads + h + 1) * HD)
        keys = [past_ref[j, :, cut] for j in range(blocks)]
        top = block_scores(q_ref[:, cut], live_ref, 0, keys, score_scr, scale)
        total = weigh(score_scr, weight_scr, top, blocks)
        values = past_ref[:, :, v_cut].reshape(blocks * past_len, HD)
        acc_ref[:, cut] = jnp.dot(weight_scr[...], values, preferred_element_type=F32)
        top_ref[:, cut] = jnp.broadcast_to(top, (q_ref.shape[0], HD))
        total_ref[:, cut] = jnp.broadcast_to(total, (q_ref.shape[0], HD))


def attend_more(heads, h, scale, live_ref, base, q_ref, kv_ref, running, score_scr, weight_scr):
    chips, tok, _ = kv_ref.shape
    cut = slice(h * HD, (h + 1) * HD)
    v_cut = slice((heads + h) * HD, (heads + h + 1) * HD)
    past_top, past_total, past_acc = [ref[:, cut] for ref in running]
    keys = [kv_ref[j, :, cut] for j in range(chips)]
    top = jnp.maximum(past_top, block_scores(q_ref[:, cut], live_ref, base, keys, score_scr, scale))
    total = weigh(score_scr, weight_scr, top, chips)
    shrink = jnp.exp(past_top - top)
    values = kv_ref[:, :, v_cut].reshape(chips * tok, HD)
    acc = past_acc * shrink + jnp.dot(weight_scr[...], values, preferred_element_type=F32)
    return top, past_total * shrink + total, acc


def near_kernel(
    heads, scale, live_ref, q_ref, near_ref, top_ref, total_ref, acc_ref, top_out, total_out, acc_out, score_scr, weight_scr
):
    running = (top_ref, total_ref, acc_ref)
    for h in range(heads):
        news = attend_more(heads, h, scale, live_ref, 0, q_ref, near_ref, running, score_scr, weight_scr)
        for ref, new in zip((top_out, total_out, acc_out), news):
            ref[:, h * HD : (h + 1) * HD] = new


def far_kernel(
    heads, scale, by_token, live_ref, place_ref, q_ref, far_ref, top_ref, total_ref, acc_ref, w_ref,
    out_ref, score_scr, weight_scr, att_scr,
):
    chips, tok, _ = far_ref.shape
    z = place_ref[0]
    n_z = out_ref.shape[0]
    rows = tok // n_z
    running = (top_ref, total_ref, acc_ref)
    for h in range(heads):
        _, total, acc = attend_more(heads, h, scale, live_ref, chips, q_ref, far_ref, running, score_scr, weight_scr)
        att_scr[:, h * HD : (h + 1) * HD] = (acc / total).astype(BF16)
    full = w_ref.shape[1]
    width = out_ref.shape[2] if not by_token else full // 16
    step = 2 * width
    for c in range(full // step):
        o = jnp.dot(att_scr[...], w_ref[:, c * step : (c + 1) * step], preferred_element_type=F32)
        if by_token:
            for r in range(n_z):
                out_ref[lax.rem(r + n_z - z, n_z), :, c * step : (c + 1) * step] = o[r * rows : (r + 1) * rows]
        else:
            o = o.T
            for half in range(2):
                block = 2 * c + half
                out_ref[lax.rem(block % n_z + n_z - z, n_z), block // n_z] = o[half * width : (half + 1) * width]


def pick_kernel(picked_ref, keys_ref, values_ref, out_ref):
    hw = keys_ref.shape[2]
    for d in range(out_ref.shape[0]):
        out_ref[d, :, :hw] = keys_ref[picked_ref[d]]
        out_ref[d, :, hw:] = values_ref[picked_ref[d]]


def modulate(wide, meansq, mod_ref, cut):
    return (wide * lax.rsqrt(meansq + 1e-06) * (1.0 + mod_ref[1:2, cut]) + mod_ref[0:1, cut]).astype(BF16)


def fetch_weights(w_key_ref, w_value_ref, k_scr, v_scr, sems):
    fetches = [
        pltpu.make_async_copy(w_key_ref, k_scr, sems.at[0]),
        pltpu.make_async_copy(w_value_ref, v_scr, sems.at[1]),
    ]
    for fetch in fetches:
        fetch.start()
    return fetches


def project(normed_scr, weights, fetches, kv_scr, kv_ref, sems):
    for i, (weight, fetch) in enumerate(zip(weights, fetches)):
        fetch.wait()
        width = weight.shape[1]
        out = jnp.dot(normed_scr[...], weight[...], preferred_element_type=F32)
        kv_scr[:, i * width : (i + 1) * width] = out.astype(BF16)
    copies = [pltpu.make_async_copy(kv_scr, kv_ref.at[c], sems.at[4 + c]) for c in range(kv_ref.shape[0])]
    for copy in copies:
        copy.start()
    return copies


def first_norm_kernel(place_ref, mod_ref, w_key_ref, w_value_ref, *refs):
    blocks, (x_out, normed_out, kv_ref, x_ref, normed_ref, turned, k_scr, v_scr, kv_scr, sems) = refs[:-10], refs[-10:]
    fetches = fetch_weights(w_key_ref, w_value_ref, k_scr, v_scr, sems)
    n_z = len(blocks)
    n_yh, width, tok = blocks[0].shape
    full = x_ref.shape[1]
    for k, block in enumerate(blocks):
        here = lax.rem(place_ref[0] + k, n_z)
        for y in range(n_yh):
            row = pl.multiple_of((lax.rem(place_ref[2] + y, n_yh) * n_z + here) * width, 64)
            turned[pl.ds(row, width), :] = block[y]
    def turn(c, squares):
        cut = pl.ds(pl.multiple_of(c * HD, HD), HD)
        wide = turned[cut, :].astype(F32).T
        x_ref[:, cut] = wide.astype(BF16)
        return squares + wide * wide

    squares = lax.fori_loop(0, full // HD, turn, jnp.zeros((tok, HD), F32), unroll=UNROLL)
    copies = [pltpu.make_async_copy(x_ref, x_out, sems.at[2])]
    copies[0].start()
    meansq = jnp.sum(squares, axis=1, keepdims=True) * (1.0 / full)
    def apply(c, _):
        cut = pl.ds(pl.multiple_of(c * HD, HD), HD)
        normed_ref[:, cut] = modulate(x_ref[:, cut].astype(F32), meansq, mod_ref, cut)
        return 0

    lax.fori_loop(0, full // HD, apply, 0, unroll=UNROLL)
    copies.append(pltpu.make_async_copy(normed_ref, normed_out, sems.at[3]))
    copies[1].start()
    copies += project(normed_ref, (k_scr, v_scr), fetches, kv_scr, kv_ref, sems)
    for copy in copies:
        copy.wait()


def second_norm_kernel(place_ref, step_ref, mod_ref, x_ref, *refs):
    blocks, (normed_ref, own_ref) = refs[:-2], refs[-2:]
    n_z = len(blocks)
    rows, full = blocks[0].shape
    width = own_ref.shape[1]
    here = place_ref[1] * width
    start = pl.multiple_of(here // HD * HD, HD)
    shift = here - start
    span = -(-width // HD) * HD
    for k, block in enumerate(blocks):
        row = pl.multiple_of(lax.rem(place_ref[0] + k, n_z) * rows, rows)
        squares = jnp.zeros((rows, HD), F32)
        for c in range(full // HD):
            cut = slice(c * HD, (c + 1) * HD)
            x = x_ref[pl.ds(row, rows), cut].astype(F32) + step_ref[0] * block[:, cut].astype(F32)
            x = x.astype(BF16)
            normed_ref[pl.ds(row, rows), cut] = x
            squares = squares + x.astype(F32) * x.astype(F32)
        meansq = jnp.sum(squares, axis=1, keepdims=True) * (1.0 / full)
        for c in range(full // HD):
            cut = slice(c * HD, (c + 1) * HD)
            x = normed_ref[pl.ds(row, rows), cut].astype(F32)
            normed_ref[pl.ds(row, rows), cut] = modulate(x, meansq, mod_ref, cut)
        window = block[:, pl.ds(start, span)].astype(F32)
        window = jnp.where(shift > 0, pltpu.roll(window, span - HD // 2, 1), window)
        own_ref[pl.ds(row, rows), :] = window[:, :width].astype(BF16)


def per_device(
    latent,
    noise_levels,
    mod_table,
    w_query,
    w_key,
    w_value,
    w_out,
    hist_keys,
    hist_values,
    frame_home,
    hist_list,
    list_count,
):
    tok, width = latent.shape
    level_count, _, full = mod_table.shape
    heads = w_query.shape[1] // HD
    hw = heads * HD
    n_ctx = lax.axis_size(CTX)
    n_chip = lax.axis_size(CHIPS)
    n_z = lax.axis_size("z")
    n_yh = lax.axis_size("yh")
    yh = lax.axis_index("yh")
    core = lax.axis_index("core")
    chip = lax.axis_index(CHIPS)
    z = lax.axis_index("z")
    rows = tok // n_z
    scale = 1.0 / math.sqrt(HD)
    down = [(i, (i - 1) % n_z) for i in range(n_z)]
    up = [(i, (i + 1) % n_z) for i in range(n_z)]

    def ring_gather(block, beside):
        got = {0: block}
        for k in range(1, n_z // 2 + 1):
            got[k] = lax.ppermute(got[k - 1], "z", down)
            if 2 * k < n_z:
                got[-k] = lax.ppermute(got[1 - k], "z", up)
            if k == 1 and beside is not None:
                got[1], got[-1], beside = lax.optimization_barrier((got[1], got[-1], beside))
        return [got[k] if 2 * k <= n_z else got[k - n_z] for k in range(n_z)], beside

    def ring_sum(parts, sent):
        low = parts[n_z // 2].astype(sent)
        high = parts[n_z // 2 - 1].astype(sent)
        for k in range(n_z // 2, 0, -1):
            low = lax.ppermute(low, "z", down)
            if 2 * k > 2:
                high = lax.ppermute(high, "z", up)
            low, high = lax.optimization_barrier((low, high))
            if k > 1:
                low = (low.astype(F32) + parts[n_z - k + 1]).astype(sent)
            if k > 2:
                high = (high.astype(F32) + parts[k - 2]).astype(sent)
        return parts[0] + low.astype(F32) + high.astype(F32)

    sigma = (noise_levels[:, 0].astype(F32) + 1.0) / level_count
    steps = sigma[1:] - sigma[:-1]

    slot_per_owner, past_len, _ = hist_keys.shape
    frames = jnp.arange(frame_home.shape[0], dtype=jnp.int32)
    wanted = jnp.sum(jnp.where(hist_list[0][:, None] == frames[None, :], frame_home[None, :], 0), axis=1)
    matched = (wanted // slot_per_owner)[:, None] == jnp.arange(n_ctx, dtype=jnp.int32)[None, :]
    request = jnp.sum(jnp.where(matched, (wanted % slot_per_owner)[:, None], 0), axis=0)
    in_list = jnp.arange(n_ctx, dtype=jnp.int32) < list_count[0]
    valid_owner = jnp.any(matched & in_list[:, None], axis=0)
    picked = lax.all_to_all(request[:, None], CTX, split_axis=0, concat_axis=0, tiled=True)[:, 0]
    own = latent.T
    other, picked = lax.optimization_barrier((lax.ppermute(own, "yh", SWAP), picked))
    smem = pl.BlockSpec(memory_space=pltpu.SMEM)
    vmem = pl.BlockSpec(memory_space=pltpu.VMEM)
    hbm = pl.BlockSpec(memory_space=pl.ANY)
    limit = pltpu.CompilerParams(vmem_limit_bytes=24 * 2**20)
    large = pltpu.CompilerParams(vmem_limit_bytes=56 * 2**20)
    asked = pl.pallas_call(
        pick_kernel,
        out_shape=jax.ShapeDtypeStruct((n_ctx, past_len, 2 * hw), BF16),
        in_specs=[smem, vmem, vmem],
        out_specs=vmem,
        compiler_params=large,
    )(picked, hist_keys, hist_values)
    pair = jnp.stack([own, other])
    blocks, asked = ring_gather(pair, asked)
    past = lax.all_to_all(asked, CTX, split_axis=0, concat_axis=0, tiled=True)

    mods = [mod_table[noise_levels[s, 0]] for s in range(2)]
    place = jnp.stack([z, lax.axis_index(TP), yh]).astype(jnp.int32)
    wide = jax.ShapeDtypeStruct((tok, full), BF16)
    kv_copies = jax.ShapeDtypeStruct((n_chip, tok, 2 * hw), BF16)
    wide_scratch = pltpu.VMEM((tok, full), BF16)
    kv_scratch = [
        pltpu.VMEM((full, hw), BF16),
        pltpu.VMEM((full, hw), BF16),
        pltpu.VMEM((tok, 2 * hw), BF16),
        pltpu.SemaphoreType.DMA((4 + n_chip,)),
    ]
    x0_full, normed, kv = pl.pallas_call(
        first_norm_kernel,
        out_shape=[wide, wide, kv_copies],
        in_specs=[smem, vmem, hbm, hbm] + [vmem] * n_z,
        out_specs=[hbm] * 3,
        scratch_shapes=[wide_scratch, wide_scratch, pltpu.VMEM((full, tok), BF16)] + kv_scratch,
        compiler_params=large,
    )(place, mods[0], w_key, w_value, *blocks)

    chips = jnp.arange(n_chip, dtype=jnp.int32)
    seen_own = chips <= chip
    seen_other = (chips < chip) | ((chips == chip) & (core == 1))
    group_live = jnp.concatenate([seen_own, seen_other]).astype(jnp.int32)
    past_live = valid_owner.astype(jnp.int32)

    def attend(normed, kv, past, by_token):
        kv, past = lax.optimization_barrier((kv, past))
        near = lax.all_to_all(kv, CHIPS, split_axis=0, concat_axis=0, tiled=True)
        q = jnp.dot(normed, w_query, preferred_element_type=F32).astype(BF16)
        stat = jax.ShapeDtypeStruct((tok, hw), F32)

        def scratch(keys):
            return [pltpu.VMEM((tok, keys), F32), pltpu.VMEM((tok, keys), BF16)]

        def cost(keys, out):
            return pl.CostEstimate(
                flops=4 * tok * keys * hw + 2 * tok * hw * out,
                bytes_accessed=8 * keys * hw * 4 + hw * out * 2 + tok * out * 2,
                transcendentals=tok * keys * heads,
            )

        past_keys, chip_keys = n_ctx * past_len, n_chip * tok
        top, total, acc = pl.pallas_call(
            functools.partial(past_kernel, heads, scale),
            out_shape=[stat, stat, stat],
            in_specs=[smem] + [vmem] * 2,
            out_specs=[vmem] * 3,
            scratch_shapes=scratch(past_keys),
            compiler_params=limit,
            cost_estimate=cost(past_keys, 0),
        )(past_live, q, past)
        near, top, total, acc = lax.optimization_barrier((near, top, total, acc))
        far = lax.ppermute(near, "core", SWAP)
        top, total, acc = pl.pallas_call(
            functools.partial(near_kernel, heads, scale),
            out_shape=[stat, stat, stat],
            in_specs=[smem] + [vmem] * 5,
            out_specs=[vmem] * 3,
            scratch_shapes=scratch(chip_keys),
            compiler_params=limit,
            cost_estimate=cost(chip_keys, 0),
        )(group_live, q, near, top, total, acc)
        return pl.pallas_call(
            functools.partial(far_kernel, heads, scale, by_token),
            out_shape=jax.ShapeDtypeStruct((n_z, rows, full) if by_token else (n_z, n_yh, width, tok), F32),
            in_specs=[smem, smem] + [vmem] * 6,
            out_specs=vmem,
            scratch_shapes=scratch(chip_keys) + [pltpu.VMEM((tok, hw), BF16)],
            compiler_params=limit,
            cost_estimate=cost(chip_keys, full),
        )(group_live, place, q, far, top, total, acc, w_out)

    part = attend(normed, kv, past, True)
    half = ring_sum([part[k] for k in range(n_z)], F32)
    rest = lax.ppermute(half, "yh", SWAP)
    v0_rows = (half + rest).astype(BF16)
    blocks, _ = ring_gather(v0_rows, None)
    normed, v0 = pl.pallas_call(
        second_norm_kernel,
        out_shape=[wide, jax.ShapeDtypeStruct((tok, width), BF16)],
        in_specs=[smem, smem] + [vmem] * (2 + n_z),
        out_specs=[vmem, vmem],
        compiler_params=limit,
        cost_estimate=pl.CostEstimate(flops=16 * tok * full, bytes_accessed=24 * 2**20, transcendentals=tok),
    )(place, steps[:1], mods[1], x0_full, *blocks)
    x1 = (latent.astype(F32) + steps[0] * v0.astype(F32)).astype(BF16)

    k = jnp.dot(normed, w_key, preferred_element_type=F32).astype(BF16)
    v = jnp.dot(normed, w_value, preferred_element_type=F32).astype(BF16)
    kv = jnp.broadcast_to(jnp.concatenate([k, v], axis=1)[None], kv_copies.shape)
    part = attend(normed, kv, past, False)
    halves = ring_sum([part[k] for k in range(n_z)], BF16)
    keep = jnp.where(yh == 1, halves[1], halves[0])
    give = jnp.where(yh == 1, halves[0], halves[1])
    rest = lax.ppermute(give, "yh", SWAP)
    v1 = (keep + rest).astype(BF16).T
    x2 = (x1.astype(F32) + steps[1] * v1.astype(F32)).astype(BF16)
    return x2, jnp.stack([v0, v1])


def solution(mesh):
    fine = Mesh(mesh.devices.reshape(2, 4, 2, 2, 8), ("yl", "x", "core", "yh", "z"))
    return jax.shard_map(
        per_device,
        mesh=fine,
        in_specs=(
            P(CTX, TP),
            P(None, CTX),
            P(),
            P(None, TP),
            P(None, TP),
            P(None, TP),
            P(TP, None),
            P(CTX, None, TP),
            P(CTX, None, TP),
            P(),
            P(CTX, None),
            P(CTX),
        ),
        out_specs=(P(CTX, TP), P(None, CTX, TP)),
        check_vma=False,
    )
```
